512 devices in a mesh: zt: 64 (over z, y), xy: 8 (over x, core).
Axes of the slice: x: 4, y: 8, z: 8, core: 2. Of those that a mesh axis runs over, the one named last changes fastest.
Arguments:
- right_side: float32 [8, 256, 96, 128], P('xy', 'zt'), may hold values from -200 to 200
- self_link: float32 [8, 256, 4, 4608], P('xy', 'zt'), may hold values from -1 to 4
- hop_links: float32 [8, 8, 256, 4, 4608], P(None, 'xy', 'zt'), may hold values from -0.3125 to 0.3125
Outputs:
- solution_field: float32 [8, 256, 96, 128], P('xy', 'zt')
- residual: float32 [8, 256, 96, 128], P('xy', 'zt')
The draws below stay inside these ranges and needn't reach their ends.
All inputs are finite; a program needn't handle non-finite values.
Results may differ from the reference program's by a relative error of at most 0.00026.
Values sent between devices are 32-bit elements; how exact they have to be, the bound alone decides.
A program may use at most 128 MiB of HBM per device.

```python
import math
import jax
import jax.numpy as jnp
from jax import lax

NV = 48
RHS = 32
NT = 32
NY = 4
NX = 8
NZ = 8


def draw_right_side(key, part):
    key = jax.random.fold_in(key, 9)
    key_base, key_site, key_column = jax.random.split(key, 3)
    shape = (NX, NZ * NT, 2 * NV, NY, RHS)
    site_scale = jnp.exp(jax.random.uniform(key_site, (NX, NZ * NT, 1, NY, 1), jnp.float32, 0.0, math.log(10.0)))
    column_scale = jnp.exp(jax.random.uniform(key_column, (RHS,), jnp.float32, 0.0, math.log(10.0)))
    rising = 3.0 ** (jnp.arange(NZ * NT, dtype=jnp.float32) / (NZ * NT))
    rising = rising[None, :, None, None, None]
    base = jnp.clip(jax.random.normal(key_base, shape, jnp.float32), -6.0, 6.0)
    values = 0.1 * base * site_scale * column_scale * rising
    return values.reshape(NX, NZ * NT, 2 * NV, NY * RHS)


def draw_self_link(key, part):
    key = jax.random.fold_in(key, 5)
    key_noise, key_diag = jax.random.split(key, 2)
    noise = jnp.clip(jax.random.normal(key_noise, (NX, NZ * NT, NY, 2, NV, NV), jnp.float32), -4.0, 4.0)
    noise = noise / jnp.sqrt(8.0 * NV)
    diagonal = jax.random.uniform(key_diag, (NX, NZ * NT, NY, NV), jnp.float32, 1.5, 2.5)
    identity = jnp.eye(NV, dtype=jnp.float32)
    real_part = noise[..., 0, :, :] + diagonal[..., :, None] * identity
    stacked = jnp.stack([real_part, noise[..., 1, :, :]], axis=-3)
    return stacked.reshape(NX, NZ * NT, NY, 2 * NV * NV)


def level_of(own_key, extent, shards, smallest, largest):
    def one(position, parts):
        heights = jax.random.uniform(jax.random.fold_in(jax.random.fold_in(own_key, 6), position), (parts,), jnp.float32, smallest / len(shards), largest / len(shards))
        return jnp.repeat(jnp.exp(heights), extent[position] // parts).reshape((-1,) + (1,) * (len(extent) - position - 1))

    gain = one(*shards[0])
    for cut in shards[1:]:
        gain = gain * one(*cut)
    return gain


def gaussian(own_key, extent, scale, bound, cuts=(), kind=jnp.bfloat16):
    gain = level_of(own_key, extent, cuts, -0.22, 0.18) if cuts else 1.0
    entries = jax.random.normal(own_key, extent, jnp.float32) * scale * gain
    return jnp.minimum(jnp.maximum(entries, -bound), bound).astype(kind)


def setup_inputs(seed: int = 0) -> dict:
    keys = jax.random.split(jax.random.key(seed), 4)
    right_side = draw_right_side(jax.random.fold_in(keys[3], 71), 0)
    self_link = draw_self_link(jax.random.fold_in(keys[3], 71), 0)
    hop_links = gaussian(keys[2], (8, NX, NZ * NT, NY, 2 * NV * NV), (8 * NV) ** -0.5, 0.3125, ((1, 8), (2, 64)), jnp.float32)
    return {"right_side": right_side, "self_link": self_link, "hop_links": hop_links}


HIGHEST = lax.Precision.HIGHEST

def block_form(packed):
    shaped = packed.reshape(packed.shape[:-1] + (2, NV, NV))
    real_part = shaped[..., 0, :, :]
    imag_part = shaped[..., 1, :, :]
    upper = jnp.concatenate([real_part, -imag_part], axis=-1)
    lower = jnp.concatenate([imag_part, real_part], axis=-1)
    return jnp.concatenate([upper, lower], axis=-2)

def hop_product(packed, field):
    split = field.reshape(field.shape[0], field.shape[1], 2 * NV, NY, RHS)
    result = jnp.einsum('xtsab,xtbsc->xtasc', block_form(packed), split, precision=HIGHEST)
    return result.reshape(field.shape)

def lattice_neighbours(field):
    shaped = field.reshape(field.shape[0], field.shape[1], 2 * NV, NY, RHS)

    def flatten(values):
        return values.reshape(field.shape)
    return [jnp.roll(field, -1, 0), jnp.roll(field, 1, 0), flatten(jnp.roll(shaped, -1, 3)), flatten(jnp.roll(shaped, 1, 3)), jnp.roll(field, -NT, 1), jnp.roll(field, NT, 1), jnp.roll(field, -1, 1), jnp.roll(field, 1, 1)]

def operator(field, self_link, hop_links):
    summed = hop_product(self_link, field)
    for index, shifted in enumerate(lattice_neighbours(field)):
        summed = summed - hop_product(hop_links[index], shifted)
    return summed

def complex_parts(field):
    shaped = field.reshape(field.shape[0], field.shape[1], 2, NV, NY, RHS)
    return (shaped[:, :, 0], shaped[:, :, 1])

def inner_local(left, right):
    left_re, left_im = complex_parts(left)
    right_re, right_im = complex_parts(right)

    def contract(first, second):
        return jnp.einsum('xtnsc,xtnsd->cd', first, second, precision=HIGHEST)
    return (contract(left_re, right_re) + contract(left_im, right_im), contract(left_re, right_im) - contract(left_im, right_re))

def gram_solve(gram, target):
    gram_re, gram_im = gram
    target_re, target_im = target
    upper = jnp.concatenate([gram_re, -gram_im], axis=1)
    lower = jnp.concatenate([gram_im, gram_re], axis=1)
    matrix = jnp.concatenate([upper, lower], axis=0)
    matrix = 0.5 * (matrix + matrix.T)
    factor = jnp.linalg.cholesky(matrix)
    solved = jax.scipy.linalg.cho_solve((factor, True), jnp.concatenate([target_re, target_im], axis=0))
    count = gram_re.shape[0]
    return (solved[:count], solved[count:])

def combine(field, coef):
    coef_re, coef_im = coef
    field_re, field_im = complex_parts(field)

    def times(values, matrix):
        return jnp.einsum('xtnsc,cd->xtnsd', values, matrix, precision=HIGHEST)
    new_re = times(field_re, coef_re) - times(field_im, coef_im)
    new_im = times(field_re, coef_im) + times(field_im, coef_re)
    return jnp.stack([new_re, new_im], axis=2).reshape(field.shape)

def reference(right_side, self_link, hop_links):
    first_image = operator(right_side, self_link, hop_links)
    first_gram = inner_local(first_image, first_image)
    first_coef = gram_solve(first_gram, inner_local(first_image, right_side))
    residual_one = right_side - combine(first_image, first_coef)
    second_image = operator(residual_one, self_link, hop_links)
    projection = gram_solve(first_gram, inner_local(first_image, second_image))
    direction_image = second_image - combine(first_image, projection)
    direction = residual_one - combine(right_side, projection)
    second_gram = inner_local(direction_image, direction_image)
    second_coef = gram_solve(second_gram, inner_local(direction_image, residual_one))
    solution_field = combine(right_side, first_coef) + combine(direction, second_coef)
    residual = residual_one - combine(direction_image, second_coef)
    return (solution_field, residual)
```

```python
import functools

import jax
import jax.numpy as jnp
from jax import lax
from jax.experimental import pallas as pl
from jax.experimental.pallas import tpu as pltpu
from jax.sharding import PartitionSpec as P

NV = 48
RHS = 32
NT = 32
NY = 4
ROWS = 4

MESH = pl.DeviceIdType.MESH
HIGHEST = lax.Precision.HIGHEST
F32 = jnp.float32
BF16 = jnp.bfloat16

HOP_OF_SLOT = (None, 2, 3, 6, 7, 0, 1, 4, 5)
SLOTS = 9
KSLOT = 256


def dot(left, right):
    return jnp.dot(left, right, precision=HIGHEST, preferred_element_type=F32)


def lane_iota(rows):
    return lax.broadcasted_iota(jnp.int32, (rows, 128), 1)


def times_minus_i(rows):
    half = rows.shape[0] // 2
    return jnp.concatenate([rows[half:], -rows[:half]], axis=0)


def field_rows(ref, first=0):
    return ref[first : first + ROWS].reshape(ROWS * 2 * NV, 128)


def field_j(rows):
    parts = []
    for t in range(ROWS):
        base = t * 2 * NV
        parts.append(rows[base + NV : base + 2 * NV])
        parts.append(-rows[base : base + NV])
    return jnp.concatenate(parts, axis=0)


def diagonal_sum(product, tile, group):
    total = None
    for y in range(NY):
        block = product[32 * y : 32 * (y + 1), 128 * tile : 128 * (tile + 1)]
        shift = (32 * (group - y)) % 128
        if shift:
            block = pltpu.roll(block, shift, 1)
        total = block if total is None else total + block
    return total


def by_group(group, parts):
    out = parts[-1]
    for index in range(len(parts) - 2, -1, -1):
        out = jnp.where(group == index, parts[index], out)
    return out


def packed_inner(product, tiles):
    group = lane_iota(32) // 32
    return by_group(group, [diagonal_sum(product, tile, g) for g, tile in enumerate(tiles)])


def eliminate(packed):
    group = lane_iota(32) // 32
    lane = lane_iota(32)
    row32 = lax.broadcasted_iota(jnp.int32, (32, 128), 0)
    eye = jnp.where(lane == row32 + 96, 1.0, 0.0).astype(F32)
    down = pltpu.roll(packed, 96, 1)
    up = pltpu.roll(packed, 32, 1)
    top = by_group(group, [packed, -packed, packed, eye])
    bottom = by_group(group, [down, up, down, jnp.zeros_like(packed)])
    work = jnp.concatenate([top, bottom], axis=0)
    row = lax.broadcasted_iota(jnp.int32, (64, 128), 0)
    for k in range(RHS):
        inverse = 1.0 / work[k : k + 1, k : k + 1]
        first = work[k : k + 1, :] * inverse
        second = work[k + 32 : k + 33, :] * inverse
        updated = work - work[:, k : k + 1] * first - work[:, k + 32 : k + 33] * second
        work = jnp.where(row == k, first, jnp.where(row == k + 32, second, updated))
    return work


def repeated(block, group_index):
    group = lane_iota(32) // 32
    block = jnp.where(group == group_index, block, 0.0)
    block = block + pltpu.roll(block, 64, 1)
    return block + pltpu.roll(block, 32, 1)


def column_matrix(coef, group_index):
    group = lane_iota(32) // 32
    real = repeated(coef[:32], group_index)
    imag = repeated(coef[32:], group_index)
    blocks = [jnp.where(group == y, real, 0.0) for y in range(NY)]
    blocks += [jnp.where(group == y, -imag, 0.0) for y in range(NY)]
    return jnp.concatenate(blocks, axis=0)


def kernel(
    sizes,
    b_ref,
    self_ref,
    hop_ref,
    sol_ref,
    res_ref,
    raw,
    rows_scr,
    amat,
    bhi,
    blo,
    ext,
    halo,
    acc,
    second,
    first_res,
    pay,
    rs_buf,
    z_buf,
    x_buf,
    ag_buf,
    link_sem,
    b_sem,
    halo_send,
    halo_recv,
    t_send,
    t_recv,
    red_send,
    red_recv,
):
    yb, zb, xb = sizes
    zt = lax.axis_index("zt")
    xy = lax.axis_index("xy")
    my_y = lax.rem(zt, yb)
    my_z = lax.div(zt, yb)
    count = yb * zb

    def zt_at(by):
        return lax.rem(zt + (by + count), count)

    def xy_at(by):
        return lax.rem(xy + (by + xb), xb)

    def link_copies(slot):
        source = self_ref.at[0] if slot == 0 else hop_ref.at[HOP_OF_SLOT[slot], 0]
        return pltpu.make_async_copy(source, raw.at[slot], link_sem.at[slot])

    own = pltpu.make_async_copy(b_ref.at[0], ext.at[0, pl.ds(1, ROWS)], b_sem)
    own.start()
    for slot in range(SLOTS):
        link_copies(slot).start()

    partners = [(zt_at(1), xy), (zt_at(-1), xy)]
    partners += [(my_z * yb + lax.rem(my_y + o, yb), xy) for o in range(1, yb)]
    partners += [(lax.rem(my_z + o, zb) * yb + my_y, xy) for o in range(1, zb)]
    partners += [(zt, lax.rem(xy + o, xb)) for o in range(1, xb)]
    barrier = pltpu.get_barrier_semaphore()
    for partner in partners:
        pl.semaphore_signal(barrier, inc=1, device_id=partner, device_id_type=MESH)
    pl.semaphore_wait(barrier, len(partners))

    targets = ((zt, xy_at(-1)), (zt, xy_at(1)), (zt_at(-yb), xy), (zt_at(yb), xy))

    def halo_copy(which, side, t):
        return pltpu.make_async_remote_copy(
            src_ref=ext.at[which, 1 + t],
            dst_ref=halo.at[which, side, t],
            send_sem=halo_send.at[which, side, t],
            recv_sem=halo_recv.at[which, side, t],
            device_id=targets[side],
            device_id_type=MESH,
        )

    def t_copy(which, side):
        return pltpu.make_async_remote_copy(
            src_ref=ext.at[which, 1 if side == 0 else ROWS],
            dst_ref=ext.at[which, ROWS + 1 if side == 0 else 0],
            send_sem=t_send.at[which, side],
            recv_sem=t_recv.at[which, side],
            device_id=(zt_at(-1) if side == 0 else zt_at(1), xy),
            device_id_type=MESH,
        )

    own.wait()
    t_copy(0, 0).start()
    t_copy(0, 1).start()

    def start_b(t, carry):
        for side in (2, 3, 0, 1):
            halo_copy(0, side, t).start()
        return carry

    lax.fori_loop(0, ROWS, start_b, 0)

    bhi[...] = jnp.zeros_like(bhi)
    blo[...] = jnp.zeros_like(blo)
    for slot in range(SLOTS):
        link_copies(slot).wait()
    lane = lane_iota(8)
    odd = lax.rem(lax.broadcasted_iota(jnp.int32, (8, 128), 0), 2) == 1

    def relayout(step, carry):
        slot = lax.div(step, 2)
        pair = lax.rem(step, 2)
        for g in range(12):
            tiles = [
                raw[slot, pl.ds(2 * pair, 2), :, 384 * g + 128 * n : 384 * g + 128 * (n + 1)].reshape(8, 128)
                for n in range(3)
            ]
            turned = [pltpu.roll(tile, 64, 1) for tile in tiles]
            tiles = [
                jnp.where(odd, jnp.where(lane < 64, turned[n - 1], turned[n]), tiles[n]) for n in range(3)
            ]
            for r in range(8):
                n, offset = divmod(48 * r, 128)
                piece = tiles[n]
                if offset:
                    piece = jnp.where(lane < offset, tiles[(n + 1) % 3], piece)
                    piece = pltpu.roll(piece, 128 - offset, 1)
                rows_scr[pl.ds(8 * g + r, 8, stride=96), :] = piece
        low = lane_iota(96) < 64
        for t in range(2):
            for h in range(2):
                base = (t * 4 + 2 * h) * 96
                values = jnp.where(low, rows_scr[base : base + 96, :], rows_scr[base + 96 : base + 192, :])
                hi = values.astype(BF16)
                lo = (values - hi.astype(F32)).astype(BF16)
                amat[2 * pair + t, slot, 0:96, 128 * h : 128 * (h + 1)] = hi
                amat[2 * pair + t, slot, 96:192, 128 * h : 128 * (h + 1)] = lo
        return carry

    lax.fori_loop(0, 2 * SLOTS, relayout, 0)

    group48 = lane_iota(48) // 32

    def put(slot, real, imag):
        for half, part in ((0, real), (1, imag)):
            hi = part.astype(BF16).astype(F32)
            lo = part - hi
            for y in range(NY):
                mask = group48 == y
                at = slice(slot * KSLOT + 64 * y, slot * KSLOT + 64 * y + 48)
                lanes = slice(128 * half, 128 * (half + 1))
                bhi[at, lanes] = jnp.where(mask, hi, 0.0).astype(BF16)
                blo[at, lanes] = jnp.where(mask, lo, 0.0).astype(BF16)

    def put_site(slot, site):
        put(slot, site[0:NV], site[NV : 2 * NV])

    def product(t, first, last):
        left = jnp.concatenate([amat[t, s] for s in range(first, last)], axis=1)
        right = slice(first * KSLOT, last * KSLOT)
        main = jnp.dot(left, bhi[right, :], preferred_element_type=F32)
        rest = jnp.dot(left[0:96], blo[right, :], preferred_element_type=F32)
        return main[0:96] + main[96:192] + rest

    def near(which):
        def body(t, carry):
            site = ext[which, 1 + t]
            put_site(0, -site)
            put_site(1, pltpu.roll(site, 96, 1))
            put_site(2, pltpu.roll(site, 32, 1))
            acc[t] = product(t, 0, 3)
            return carry

        lax.fori_loop(0, ROWS, body, 0)

    def far(which, out):
        t_copy(which, 0).wait_recv()
        t_copy(which, 1).wait_recv()

        def body(t, carry):
            for side in range(4):
                halo_copy(which, side, t).wait_recv()
            put_site(3, ext[which, 2 + t])
            put_site(4, ext[which, t])
            for side in range(4):
                put_site(5 + side, halo[which, side, t])
            total = acc[t] + product(t, 3, SLOTS)
            real = total[48:96, 128:256] - total[0:48, 0:128]
            imag = -(total[48:96, 0:128] + total[0:48, 128:256])
            out(t, real, imag)
            return carry

        lax.fori_loop(0, ROWS, body, 0)

    def image_out(t, real, imag):
        ext[1, 1 + t, 0:NV, :] = real
        ext[1, 1 + t, NV : 2 * NV, :] = imag
        for side in (2, 3, 0, 1):
            halo_copy(1, side, t).start()

    near(0)
    far(0, image_out)
    t_copy(1, 0).start()
    t_copy(1, 1).start()

    piece = 64 // yb

    def exchange(red, phase, buffer, me, size, source, device):
        def copy(o):
            return pltpu.make_async_remote_copy(
                src_ref=source(lax.rem(me + o, size)),
                dst_ref=buffer.at[red, me],
                send_sem=red_send.at[red, phase, o],
                recv_sem=red_recv.at[red, phase, me],
                device_id=device(lax.rem(me + o, size)),
                device_id_type=MESH,
            )

        def arrival(o):
            other = lax.rem(me + o, size)
            return pltpu.make_async_remote_copy(
                src_ref=source(other),
                dst_ref=buffer.at[red, other],
                send_sem=red_send.at[red, phase, o],
                recv_sem=red_recv.at[red, phase, other],
                device_id=device(other),
                device_id_type=MESH,
            )

        def start():
            for o in range(1, size):
                copy(o).start()

        def wait():
            for o in range(1, size):
                arrival(o).wait_recv()

        def drain():
            for o in range(1, size):
                copy(o).wait_send()

        return start, wait, drain

    def y_device(other):
        return (my_z * yb + other, xy)

    def z_device(other):
        return (other * yb + my_y, xy)

    def x_device(other):
        return (zt, other)

    def reduction(red):
        scatter = exchange(red, 0, rs_buf, my_y, yb, lambda other: pay.at[red, other], y_device)
        along_z = exchange(red, 1, z_buf, my_z, zb, lambda other: z_buf.at[red, my_z], z_device)
        along_x = exchange(red, 2, x_buf, xy, xb, lambda other: x_buf.at[red, xy], x_device)
        gather = exchange(red, 3, ag_buf, my_y, yb, lambda other: ag_buf.at[red, my_y], y_device)

        def summed(buffer, size):
            total = buffer[red, 0]
            for n in range(1, size):
                total = total + buffer[red, n]
            return total

        def step0(values):
            for n in range(yb):
                pay[red, n] = values[n * piece : (n + 1) * piece]
            rs_buf[red, my_y] = pay[red, my_y]
            scatter[0]()

        def step1():
            scatter[1]()
            z_buf[red, my_z] = summed(rs_buf, yb)
            along_z[0]()

        def step2():
            along_z[1]()
            x_buf[red, xy] = summed(z_buf, zb)
            along_x[0]()

        def step3():
            along_x[1]()
            ag_buf[red, my_y] = summed(x_buf, xb)
            gather[0]()

        def step4():
            gather[1]()
            return jnp.concatenate([ag_buf[red, n] for n in range(yb)], axis=0)

        def drain():
            for part in (scatter, along_z, along_x, gather):
                part[2]()

        return step0, step1, step2, step3, step4, drain

    red1 = reduction(0)
    red2 = reduction(1)

    rhs_rows = field_rows(ext.at[0], 1)
    image_rows = field_rows(ext.at[1], 1)
    columns = jnp.concatenate([image_rows, field_j(image_rows), rhs_rows, field_j(rhs_rows)], axis=1)
    inner = dot(image_rows.T, columns)
    packed = packed_inner(inner, (0, 1, 2, 3))
    red1[0](jnp.concatenate([packed, jnp.zeros_like(packed)], axis=0))

    near(1)
    red1[1]()

    def twice_out(t, real, imag):
        second[t, 0:NV, :] = real
        second[t, NV : 2 * NV, :] = imag

    red1[2]()
    far(1, twice_out)
    red1[3]()
    gram = red1[4]()[0:32]
    solved = eliminate(gram)

    coef1 = column_matrix(solved, 2)
    image_rows = field_rows(ext.at[1], 1)
    image_j = field_j(image_rows)
    residual_rows = field_rows(ext.at[0], 1) - dot(jnp.concatenate([image_rows, image_j], axis=1), coef1)
    twice_rows = field_rows(second)
    second_rows = image_rows - dot(jnp.concatenate([twice_rows, field_j(twice_rows)], axis=1), coef1)
    first_res[...] = residual_rows.reshape(ROWS, 2 * NV, 128)
    second[...] = second_rows.reshape(ROWS, 2 * NV, 128)

    columns = jnp.concatenate(
        [second_rows, field_j(second_rows), residual_rows, field_j(residual_rows)], axis=1
    )
    with_image = dot(image_rows.T, columns)
    with_second = dot(second_rows.T, columns)
    group = lane_iota(32) // 32
    first_pack = packed_inner(with_image, (0, 1, 2, 3))
    second_pack = packed_inner(with_second, (0, 1, 2, 3))
    red2[0](
        jnp.concatenate(
            [
                jnp.where(group < 2, first_pack, second_pack),
                jnp.where(group < 2, second_pack, first_pack),
            ],
            axis=0,
        )
    )

    zero32 = jnp.zeros((32, 128), F32)

    def real_form(real, imag):
        top = by_group(group, [real, -pltpu.roll(imag, 32, 1), zero32, zero32])
        bottom = by_group(group, [imag, pltpu.roll(real, 32, 1), zero32, zero32])
        return jnp.concatenate([top, bottom], axis=0)

    gram_form = real_form(gram, pltpu.roll(gram, 96, 1))
    inverse_form = real_form(pltpu.roll(solved[:32], 32, 1), pltpu.roll(solved[32:], 32, 1))

    def times(form, stacked):
        return dot(form[:, 0:64], stacked)

    red2[1]()
    red2[2]()
    red2[3]()
    reduced = red2[4]()
    upper, lower = reduced[:32], reduced[32:]
    group64 = lane_iota(64) // 32
    cross = jnp.where(group64 == 0, jnp.concatenate([upper, pltpu.roll(upper, 96, 1)], axis=0), 0.0)
    aside = jnp.where(
        group64 == 0, jnp.concatenate([pltpu.roll(lower, 64, 1), pltpu.roll(lower, 32, 1)], axis=0), 0.0
    )
    projection = times(inverse_form, cross)
    excess = times(gram_form, projection) - cross
    left = projection + pltpu.roll(cross, 32, 1)
    right = jnp.concatenate(
        [
            excess
            + pltpu.roll(times_minus_i(excess), 32, 1)
            + pltpu.roll(aside, 64, 1)
            + pltpu.roll(times_minus_i(aside), 96, 1),
            projection + pltpu.roll(times_minus_i(projection), 32, 1),
        ],
        axis=1,
    )
    inner = dot(left.T, right)
    packed = jnp.where(
        group < 2,
        lower - inner[32:64, 128:256] + inner[0:32, 0:128],
        upper - inner[0:32, 0:128],
    )
    solved2 = eliminate(packed)

    projection_form = real_form(projection[:32], projection[32:])
    follow = times(projection_form, solved2)
    coef2 = column_matrix(solved2, 2)
    coef_follow = column_matrix(follow, 2)
    coef_right = column_matrix(solved - follow, 2)
    rhs_rows = field_rows(ext.at[0], 1)
    image_rows = field_rows(ext.at[1], 1)
    residual_rows = field_rows(first_res)
    second_rows = field_rows(second)
    answer = dot(
        jnp.concatenate([rhs_rows, field_j(rhs_rows), residual_rows, field_j(residual_rows)], axis=1),
        jnp.concatenate([coef_right, coef2], axis=0),
    )
    sol_ref[0] = answer.reshape(ROWS, 2 * NV, 128)
    change = dot(
        jnp.concatenate([second_rows, field_j(second_rows), image_rows, field_j(image_rows)], axis=1),
        jnp.concatenate([-coef2, coef_follow], axis=0),
    )
    res_ref[0] = (residual_rows + change).reshape(ROWS, 2 * NV, 128)

    for which in range(2):
        t_copy(which, 0).wait_send()
        t_copy(which, 1).wait_send()

    def drain(t, carry):
        for which in range(2):
            for side in range(4):
                halo_copy(which, side, t).wait_send()
        return carry

    lax.fori_loop(0, ROWS, drain, 0)
    red1[5]()
    red2[5]()


def solution(mesh):
    yb = NT // ROWS
    zb = mesh.shape["zt"] // yb
    xb = mesh.shape["xy"]
    piece = 64 // yb
    block = jax.ShapeDtypeStruct((1, ROWS, 2 * NV, 128), F32)

    def local(right_side, self_link, hop_links):
        any_space = pl.BlockSpec(memory_space=pl.ANY)
        in_vmem = pl.BlockSpec(memory_space=pltpu.VMEM)
        return pl.pallas_call(
            functools.partial(kernel, (yb, zb, xb)),
            out_shape=(block, block),
            in_specs=[any_space, any_space, any_space],
            out_specs=(in_vmem, in_vmem),
            scratch_shapes=[
                pltpu.VMEM((SLOTS, ROWS, NY, 2 * NV * NV), F32),
                pltpu.VMEM((8 * 96, 128), F32),
                pltpu.VMEM((ROWS, SLOTS, 192, KSLOT), BF16),
                pltpu.VMEM((SLOTS * KSLOT, 256), BF16),
                pltpu.VMEM((SLOTS * KSLOT, 256), BF16),
                pltpu.VMEM((2, ROWS + 2, 2 * NV, 128), F32),
                pltpu.VMEM((2, 4, ROWS, 2 * NV, 128), F32),
                pltpu.VMEM((ROWS, 96, 256), F32),
                pltpu.VMEM((ROWS, 2 * NV, 128), F32),
                pltpu.VMEM((ROWS, 2 * NV, 128), F32),
                pltpu.VMEM((2, yb, piece, 128), F32),
                pltpu.VMEM((2, yb, piece, 128), F32),
                pltpu.VMEM((2, zb, piece, 128), F32),
                pltpu.VMEM((2, xb, piece, 128), F32),
                pltpu.VMEM((2, yb, piece, 128), F32),
                pltpu.SemaphoreType.DMA((SLOTS,)),
                pltpu.SemaphoreType.DMA,
                pltpu.SemaphoreType.DMA((2, 4, ROWS)),
                pltpu.SemaphoreType.DMA((2, 4, ROWS)),
                pltpu.SemaphoreType.DMA((2, 2)),
                pltpu.SemaphoreType.DMA((2, 2)),
                pltpu.SemaphoreType.DMA((2, 4, 8)),
                pltpu.SemaphoreType.DMA((2, 4, 8)),
            ],
            compiler_params=pltpu.CompilerParams(
                collective_id=0, has_side_effects=True, vmem_limit_bytes=48 * 1024 * 1024
            ),
            name="two_gcr_iterations",
        )(right_side, self_link, hop_links)

    return jax.shard_map(
        local,
        mesh=mesh,
        in_specs=(
            P("xy", "zt", None, None),
            P("xy", "zt", None, None),
            P(None, "xy", "zt", None, None),
        ),
        out_specs=(P("xy", "zt", None, None), P("xy", "zt", None, None)),
        check_vma=False,
    )
```

```python
import functools

import jax
import jax.numpy as jnp
from jax import lax
from jax.experimental import pallas as pl
from jax.experimental.pallas import tpu as pltpu
from jax.sharding import PartitionSpec as P

NV = 48
RHS = 32
NT = 32
NY = 4
ROWS = 4

MESH = pl.DeviceIdType.MESH
HIGHEST = lax.Precision.HIGHEST
F32 = jnp.float32
BF16 = jnp.bfloat16

HOP_OF_SLOT = (None, 2, 3, 6, 7, 0, 1, 4, 5)
SLOTS = 9
KSLOT = 256


def dot(left, right):
    return jnp.dot(left, right, precision=HIGHEST, preferred_element_type=F32)


def lane_iota(rows):
    return lax.broadcasted_iota(jnp.int32, (rows, 128), 1)


def times_minus_i(rows):
    half = rows.shape[0] // 2
    return jnp.concatenate([rows[half:], -rows[:half]], axis=0)


def field_rows(ref, first=0):
    return ref[first : first + ROWS].reshape(ROWS * 2 * NV, 128)


def field_j(rows):
    parts = []
    for t in range(ROWS):
        base = t * 2 * NV
        parts.append(rows[base + NV : base + 2 * NV])
        parts.append(-rows[base : base + NV])
    return jnp.concatenate(parts, axis=0)


def diagonal_sum(product, tile, group):
    total = None
    for y in range(NY):
        block = product[32 * y : 32 * (y + 1), 128 * tile : 128 * (tile + 1)]
        shift = (32 * (group - y)) % 128
        if shift:
            block = pltpu.roll(block, shift, 1)
        total = block if total is None else total + block
    return total


def by_group(group, parts):
    out = parts[-1]
    for index in range(len(parts) - 2, -1, -1):
        out = jnp.where(group == index, parts[index], out)
    return out


def packed_inner(product, tiles):
    group = lane_iota(32) // 32
    return by_group(group, [diagonal_sum(product, tile, g) for g, tile in enumerate(tiles)])


def eliminate(packed):
    group = lane_iota(32) // 32
    lane = lane_iota(32)
    row32 = lax.broadcasted_iota(jnp.int32, (32, 128), 0)
    eye = jnp.where(lane == row32 + 96, 1.0, 0.0).astype(F32)
    down = pltpu.roll(packed, 96, 1)
    up = pltpu.roll(packed, 32, 1)
    top = by_group(group, [packed, -packed, packed, eye])
    bottom = by_group(group, [down, up, down, jnp.zeros_like(packed)])
    work = jnp.concatenate([top, bottom], axis=0)
    row = lax.broadcasted_iota(jnp.int32, (64, 128), 0)
    for k in range(RHS):
        inverse = 1.0 / work[k : k + 1, k : k + 1]
        first = work[k : k + 1, :] * inverse
        second = work[k + 32 : k + 33, :] * inverse
        updated = work - work[:, k : k + 1] * first - work[:, k + 32 : k + 33] * second
        work = jnp.where(row == k, first, jnp.where(row == k + 32, second, updated))
    return work


def repeated(block, group_index):
    group = lane_iota(32) // 32
    block = jnp.where(group == group_index, block, 0.0)
    block = block + pltpu.roll(block, 64, 1)
    return block + pltpu.roll(block, 32, 1)


def column_matrix(coef, group_index):
    group = lane_iota(32) // 32
    real = repeated(coef[:32], group_index)
    imag = repeated(coef[32:], group_index)
    blocks = [jnp.where(group == y, real, 0.0) for y in range(NY)]
    blocks += [jnp.where(group == y, -imag, 0.0) for y in range(NY)]
    return jnp.concatenate(blocks, axis=0)


def kernel(
    sizes,
    b_ref,
    self_ref,
    hop_ref,
    sol_ref,
    res_ref,
    raw,
    rows_scr,
    amat,
    bhi,
    blo,
    ext,
    halo,
    acc,
    second,
    pay,
    rs_buf,
    y_buf,
    z_buf,
    ag_buf,
    link_sem,
    b_sem,
    halo_send,
    halo_recv,
    t_send,
    t_recv,
    red_send,
    red_recv,
):
    yb, zb, xb = sizes
    zt = lax.axis_index("zt")
    xy = lax.axis_index("xy")
    my_y = lax.rem(zt, yb)
    my_z = lax.div(zt, yb)
    count = yb * zb

    def zt_at(by):
        return lax.rem(zt + (by + count), count)

    def xy_at(by):
        return lax.rem(xy + (by + xb), xb)

    def link_copies(slot):
        source = self_ref.at[0] if slot == 0 else hop_ref.at[HOP_OF_SLOT[slot], 0]
        return pltpu.make_async_copy(source, raw.at[slot], link_sem.at[slot])

    own = pltpu.make_async_copy(b_ref.at[0], ext.at[0, pl.ds(1, ROWS)], b_sem)
    own.start()
    for slot in range(SLOTS):
        link_copies(slot).start()

    partners = [(zt_at(1), xy), (zt_at(-1), xy)]
    partners += [(my_z * yb + lax.rem(my_y + o, yb), xy) for o in range(1, yb)]
    partners += [(lax.rem(my_z + o, zb) * yb + my_y, xy) for o in range(1, zb)]
    partners += [(zt, lax.rem(xy + o, xb)) for o in range(1, xb)]
    barrier = pltpu.get_barrier_semaphore()
    for partner in partners:
        pl.semaphore_signal(barrier, inc=1, device_id=partner, device_id_type=MESH)
    pl.semaphore_wait(barrier, len(partners))

    targets = ((zt, xy_at(-1)), (zt, xy_at(1)), (zt_at(-yb), xy), (zt_at(yb), xy))

    def halo_copy(which, side, t):
        return pltpu.make_async_remote_copy(
            src_ref=ext.at[which, 1 + t],
            dst_ref=halo.at[which, side, t],
            send_sem=halo_send.at[which, side, t],
            recv_sem=halo_recv.at[which, side, t],
            device_id=targets[side],
            device_id_type=MESH,
        )

    def t_copy(which, side):
        return pltpu.make_async_remote_copy(
            src_ref=ext.at[which, 1 if side == 0 else ROWS],
            dst_ref=ext.at[which, ROWS + 1 if side == 0 else 0],
            send_sem=t_send.at[which, side],
            recv_sem=t_recv.at[which, side],
            device_id=(zt_at(-1) if side == 0 else zt_at(1), xy),
            device_id_type=MESH,
        )

    own.wait()
    t_copy(0, 0).start()
    t_copy(0, 1).start()

    def start_b(t, carry):
        for side in (2, 3, 0, 1):
            halo_copy(0, side, t).start()
        return carry

    lax.fori_loop(0, ROWS, start_b, 0)

    bhi[...] = jnp.zeros_like(bhi)
    blo[...] = jnp.zeros_like(blo)
    for slot in range(SLOTS):
        link_copies(slot).wait()
    lane = lane_iota(8)
    odd = lax.rem(lax.broadcasted_iota(jnp.int32, (8, 128), 0), 2) == 1

    def relayout(step, carry):
        slot = lax.div(step, 2)
        pair = lax.rem(step, 2)
        for g in range(12):
            tiles = [
                raw[slot, pl.ds(2 * pair, 2), :, 384 * g + 128 * n : 384 * g + 128 * (n + 1)].reshape(8, 128)
                for n in range(3)
            ]
            turned = [pltpu.roll(tile, 64, 1) for tile in tiles]
            tiles = [
                jnp.where(odd, jnp.where(lane < 64, turned[n - 1], turned[n]), tiles[n]) for n in range(3)
            ]
            for r in range(8):
                n, offset = divmod(48 * r, 128)
                piece = tiles[n]
                if offset:
                    piece = jnp.where(lane < offset, tiles[(n + 1) % 3], piece)
                    piece = pltpu.roll(piece, 128 - offset, 1)
                rows_scr[pl.ds(8 * g + r, 8, stride=96), :] = piece
        low = lane_iota(96) < 64
        for t in range(2):
            for h in range(2):
                base = (t * 4 + 2 * h) * 96
                values = jnp.where(low, rows_scr[base : base + 96, :], rows_scr[base + 96 : base + 192, :])
                hi = values.astype(BF16)
                lo = (values - hi.astype(F32)).astype(BF16)
                amat[2 * pair + t, slot, 0:96, 128 * h : 128 * (h + 1)] = hi
                amat[2 * pair + t, slot, 96:192, 128 * h : 128 * (h + 1)] = lo
        return carry

    lax.fori_loop(0, 2 * SLOTS, relayout, 0)

    group48 = lane_iota(48) // 32

    def put(slot, real, imag):
        for half, part in ((0, real), (1, imag)):
            hi = part.astype(BF16).astype(F32)
            lo = part - hi
            for y in range(NY):
                mask = group48 == y
                at = slice(slot * KSLOT + 64 * y, slot * KSLOT + 64 * y + 48)
                lanes = slice(128 * half, 128 * (half + 1))
                bhi[at, lanes] = jnp.where(mask, hi, 0.0).astype(BF16)
                blo[at, lanes] = jnp.where(mask, lo, 0.0).astype(BF16)

    def put_site(slot, site):
        put(slot, site[0:NV], site[NV : 2 * NV])

    def product(t, first, last):
        left = jnp.concatenate([amat[t, s] for s in range(first, last)], axis=1)
        right = slice(first * KSLOT, last * KSLOT)
        main = jnp.dot(left, bhi[right, :], preferred_element_type=F32)
        rest = jnp.dot(left[0:96], blo[right, :], preferred_element_type=F32)
        return main[0:96] + main[96:192] + rest

    def near(which):
        def body(t, carry):
            site = ext[which, 1 + t]
            put_site(0, -site)
            put_site(1, pltpu.roll(site, 96, 1))
            put_site(2, pltpu.roll(site, 32, 1))
            acc[t] = product(t, 0, 3)
            return carry

        lax.fori_loop(0, ROWS, body, 0)

    def far(which, out):
        t_copy(which, 0).wait_recv()
        t_copy(which, 1).wait_recv()

        def body(t, carry):
            for side in range(4):
                halo_copy(which, side, t).wait_recv()
            put_site(3, ext[which, 2 + t])
            put_site(4, ext[which, t])
            for side in range(4):
                put_site(5 + side, halo[which, side, t])
            total = acc[t] + product(t, 3, SLOTS)
            real = total[48:96, 128:256] - total[0:48, 0:128]
            imag = -(total[48:96, 0:128] + total[0:48, 128:256])
            out(t, real, imag)
            return carry

        lax.fori_loop(0, ROWS, body, 0)

    def image_out(t, real, imag):
        ext[1, 1 + t, 0:NV, :] = real
        ext[1, 1 + t, NV : 2 * NV, :] = imag
        for side in (2, 3, 0, 1):
            halo_copy(1, side, t).start()

    near(0)
    far(0, image_out)
    t_copy(1, 0).start()
    t_copy(1, 1).start()

    piece = 64 // xb

    def exchange(red, phase, buffer, me, size, source, device):
        def copy(o):
            return pltpu.make_async_remote_copy(
                src_ref=source(lax.rem(me + o, size)),
                dst_ref=buffer.at[red, me],
                send_sem=red_send.at[red, phase, o],
                recv_sem=red_recv.at[red, phase, me],
                device_id=device(lax.rem(me + o, size)),
                device_id_type=MESH,
            )

        def arrival(o):
            other = lax.rem(me + o, size)
            return pltpu.make_async_remote_copy(
                src_ref=source(other),
                dst_ref=buffer.at[red, other],
                send_sem=red_send.at[red, phase, o],
                recv_sem=red_recv.at[red, phase, other],
                device_id=device(other),
                device_id_type=MESH,
            )

        def start():
            for o in range(1, size):
                copy(o).start()

        def wait():
            for o in range(1, size):
                arrival(o).wait_recv()

        def drain():
            for o in range(1, size):
                copy(o).wait_send()

        return start, wait, drain

    def y_device(other):
        return (my_z * yb + other, xy)

    def z_device(other):
        return (other * yb + my_y, xy)

    def x_device(other):
        return (zt, other)

    def reduction(red):
        scatter = exchange(red, 0, rs_buf, xy, xb, lambda other: pay.at[red, other], x_device)
        along_y = exchange(red, 1, y_buf, my_y, yb, lambda other: y_buf.at[red, my_y], y_device)
        along_z = exchange(red, 2, z_buf, my_z, zb, lambda other: z_buf.at[red, my_z], z_device)
        gather = exchange(red, 3, ag_buf, xy, xb, lambda other: ag_buf.at[red, xy], x_device)

        def summed(buffer, size):
            total = buffer[red, 0]
            for n in range(1, size):
                total = total + buffer[red, n]
            return total

        def step0(values):
            for n in range(xb):
                pay[red, n] = values[n * piece : (n + 1) * piece]
            rs_buf[red, xy] = pay[red, xy]
            scatter[0]()

        def step1():
            scatter[1]()
            y_buf[red, my_y] = summed(rs_buf, xb)
            along_y[0]()

        def step2():
            along_y[1]()
            z_buf[red, my_z] = summed(y_buf, yb)
            along_z[0]()

        def step3():
            along_z[1]()
            ag_buf[red, xy] = summed(z_buf, zb)
            gather[0]()

        def step4():
            gather[1]()
            return jnp.concatenate([ag_buf[red, n] for n in range(xb)], axis=0)

        def drain():
            for part in (scatter, along_y, along_z, gather):
                part[2]()

        return step0, step1, step2, step3, step4, drain

    red1 = reduction(0)
    red2 = reduction(1)
    group = lane_iota(32) // 32
    group64 = lane_iota(64) // 32
    zero32 = jnp.zeros((32, 128), F32)

    rhs_rows = field_rows(ext.at[0], 1)
    rhs_pair = jnp.concatenate([rhs_rows, field_j(rhs_rows)], axis=1)
    image_rows = field_rows(ext.at[1], 1)
    image_pair = jnp.concatenate([image_rows, field_j(image_rows)], axis=1)
    inner = dot(image_rows.T, jnp.concatenate([image_pair, rhs_pair], axis=1))
    packed = packed_inner(inner, (0, 1, 2, 3))
    red1[0](jnp.concatenate([packed, zero32], axis=0))

    near(1)
    red1[1]()

    def twice_out(t, real, imag):
        second[t, 0:NV, :] = real
        second[t, NV : 2 * NV, :] = imag

    far(1, twice_out)

    rhs_rows = field_rows(ext.at[0], 1)
    rhs_pair = jnp.concatenate([rhs_rows, field_j(rhs_rows)], axis=1)
    image_rows = field_rows(ext.at[1], 1)
    image_pair = jnp.concatenate([image_rows, field_j(image_rows)], axis=1)
    twice_rows = field_rows(second)
    twice_pair = jnp.concatenate([twice_rows, field_j(twice_rows)], axis=1)
    with_image = dot(image_rows.T, twice_pair)
    with_twice = dot(twice_rows.T, jnp.concatenate([image_pair, twice_pair, rhs_pair], axis=1))
    with_both = jnp.concatenate([with_image, with_twice[:, 0:256]], axis=1)
    red2[0](
        jnp.concatenate(
            [packed_inner(with_both, (0, 1, 2, 3)), packed_inner(with_twice, (2, 3, 4, 5))], axis=0
        )
    )

    def real_form(real, imag):
        top = by_group(group, [real, -pltpu.roll(imag, 32, 1), zero32, zero32])
        bottom = by_group(group, [imag, pltpu.roll(real, 32, 1), zero32, zero32])
        return jnp.concatenate([top, bottom], axis=0)

    def stacked(packed, first):
        turns = [pltpu.roll(packed, (128 - 32 * g) % 128, 1) if g else packed for g in (first, first + 1)]
        return jnp.where(group64 == 0, jnp.concatenate(turns, axis=0), 0.0)

    def form_of(column):
        return real_form(column[:32], column[32:])

    red1[2]()
    red2[1]()
    red1[3]()
    red2[2]()
    gram = red1[4]()[0:32]
    solved = eliminate(gram)
    gram_column = stacked(gram, 0)
    gram_form = form_of(gram_column)
    target_column = stacked(gram, 2)
    coef1 = jnp.where(group64 == 0, pltpu.roll(solved, 64, 1), 0.0)
    inverse_form = form_of(pltpu.roll(solved, 32, 1))
    coef1_form = form_of(coef1)
    red2[3]()
    reduced = red2[4]()
    upper, lower = reduced[:32], reduced[32:]

    cross_form = form_of(stacked(upper, 0))
    image_part = gram_column - dot(cross_form[:, 0:64], coef1)
    projection = dot(inverse_form[:, 0:64], image_part)
    row64 = lax.broadcasted_iota(jnp.int32, (64, 128), 0)
    identity = jnp.where(lane_iota(64) == row64, jnp.where(group64 == 0, 1.0, 0.0), 0.0).astype(F32)
    keep = identity - projection

    grams = jnp.concatenate(
        [
            gram_form + pltpu.roll(cross_form, 64, 1),
            form_of(stacked(upper, 2)) + pltpu.roll(form_of(stacked(lower, 0)), 64, 1),
        ],
        axis=0,
    )
    weights = jnp.concatenate([keep, -coef1], axis=0)
    applied = dot(grams, weights - jnp.concatenate([pltpu.roll(coef1, 64, 1), jnp.zeros_like(coef1)], axis=0))
    targets12 = jnp.concatenate([target_column, stacked(lower, 2)], axis=0)
    applied = applied + pltpu.roll(targets12, 64, 1)
    turned = jnp.concatenate([times_minus_i(applied[:64]), times_minus_i(applied[64:])], axis=0)
    applied = applied + pltpu.roll(turned, 32, 1)
    solved2 = eliminate(dot(weights.T, applied)[0:32])

    follow = dot(jnp.concatenate([form_of(keep), coef1_form], axis=0)[:, 0:64], solved2)
    step_a = column_matrix(pltpu.roll(coef1, 64, 1) + follow[:64], 2)
    step_e = column_matrix(follow[64:], 2)
    rhs_rows = field_rows(ext.at[0], 1)
    rhs_pair = jnp.concatenate([rhs_rows, field_j(rhs_rows)], axis=1)
    image_rows = field_rows(ext.at[1], 1)
    image_pair = jnp.concatenate([image_rows, field_j(image_rows)], axis=1)
    twice_rows = field_rows(second)
    twice_pair = jnp.concatenate([twice_rows, field_j(twice_rows)], axis=1)
    answer = dot(jnp.concatenate([rhs_pair, image_pair], axis=1), jnp.concatenate([step_a, -step_e], axis=0))
    sol_ref[0] = answer.reshape(ROWS, 2 * NV, 128)
    change = dot(jnp.concatenate([image_pair, twice_pair], axis=1), jnp.concatenate([-step_a, step_e], axis=0))
    res_ref[0] = (rhs_rows + change).reshape(ROWS, 2 * NV, 128)

    for which in range(2):
        t_copy(which, 0).wait_send()
        t_copy(which, 1).wait_send()

    def drain(t, carry):
        for which in range(2):
            for side in range(4):
                halo_copy(which, side, t).wait_send()
        return carry

    lax.fori_loop(0, ROWS, drain, 0)
    red1[5]()
    red2[5]()


def solution(mesh):
    yb = NT // ROWS
    zb = mesh.shape["zt"] // yb
    xb = mesh.shape["xy"]
    piece = 64 // xb
    block = jax.ShapeDtypeStruct((1, ROWS, 2 * NV, 128), F32)

    def local(right_side, self_link, hop_links):
        in_hbm = pl.BlockSpec(memory_space=pltpu.HBM)
        in_vmem = pl.BlockSpec(memory_space=pltpu.VMEM)
        return pl.pallas_call(
            functools.partial(kernel, (yb, zb, xb)),
            out_shape=(block, block),
            in_specs=[in_hbm, in_hbm, in_hbm],
            out_specs=(in_vmem, in_vmem),
            scratch_shapes=[
                pltpu.VMEM((SLOTS, ROWS, NY, 2 * NV * NV), F32),
                pltpu.VMEM((8 * 96, 128), F32),
                pltpu.VMEM((ROWS, SLOTS, 192, KSLOT), BF16),
                pltpu.VMEM((SLOTS * KSLOT, 256), BF16),
                pltpu.VMEM((SLOTS * KSLOT, 256), BF16),
                pltpu.VMEM((2, ROWS + 2, 2 * NV, 128), F32),
                pltpu.VMEM((2, 4, ROWS, 2 * NV, 128), F32),
                pltpu.VMEM((ROWS, 96, 256), F32),
                pltpu.VMEM((ROWS, 2 * NV, 128), F32),
                pltpu.VMEM((2, xb, piece, 128), F32),
                pltpu.VMEM((2, xb, piece, 128), F32),
                pltpu.VMEM((2, yb, piece, 128), F32),
                pltpu.VMEM((2, zb, piece, 128), F32),
                pltpu.VMEM((2, xb, piece, 128), F32),
                pltpu.SemaphoreType.DMA((SLOTS,)),
                pltpu.SemaphoreType.DMA,
                pltpu.SemaphoreType.DMA((2, 4, ROWS)),
                pltpu.SemaphoreType.DMA((2, 4, ROWS)),
                pltpu.SemaphoreType.DMA((2, 2)),
                pltpu.SemaphoreType.DMA((2, 2)),
                pltpu.SemaphoreType.DMA((2, 4, 8)),
                pltpu.SemaphoreType.DMA((2, 4, 8)),
            ],
            compiler_params=pltpu.CompilerParams(
                collective_id=0, has_side_effects=True, vmem_limit_bytes=48 * 1024 * 1024
            ),
            name="two_gcr_iterations",
        )(*[pltpu.with_memory_space_constraint(x, pltpu.HBM) for x in (right_side, self_link, hop_links)])

    return jax.shard_map(
        local,
        mesh=mesh,
        in_specs=(
            P("xy", "zt", None, None),
            P("xy", "zt", None, None),
            P(None, "xy", "zt", None, None),
        ),
        out_specs=(P("xy", "zt", None, None), P("xy", "zt", None, None)),
        check_vma=False,
    )
```

```python
import functools

import jax
import jax.numpy as jnp
from jax import lax
from jax.experimental import pallas as pl
from jax.experimental.pallas import tpu as pltpu
from jax.sharding import PartitionSpec as P

NV = 48
RHS = 32
NT = 32
NY = 4
ROWS = 4

MESH = pl.DeviceIdType.MESH
HIGHEST = lax.Precision.HIGHEST
F32 = jnp.float32
BF16 = jnp.bfloat16

HOP_OF_SLOT = (None, 2, 3, 6, 7, 0, 1, 4, 5)
SLOTS = 9
KSLOT = 256
PITCH = 97


def dot(left, right):
    return jnp.dot(left, right, precision=HIGHEST, preferred_element_type=F32)


def lane_iota(rows):
    return lax.broadcasted_iota(jnp.int32, (rows, 128), 1)


def times_minus_i(rows):
    half = rows.shape[0] // 2
    return jnp.concatenate([rows[half:], -rows[:half]], axis=0)


def field_rows(ref, first=0):
    return ref[first : first + ROWS].reshape(ROWS * 2 * NV, 128)


def field_j(rows):
    parts = []
    for t in range(ROWS):
        base = t * 2 * NV
        parts.append(rows[base + NV : base + 2 * NV])
        parts.append(-rows[base : base + NV])
    return jnp.concatenate(parts, axis=0)


def diagonal_sum(product, tile, group):
    total = None
    for y in range(NY):
        block = product[32 * y : 32 * (y + 1), 128 * tile : 128 * (tile + 1)]
        shift = (32 * (group - y)) % 128
        if shift:
            block = pltpu.roll(block, shift, 1)
        total = block if total is None else total + block
    return total


def by_group(group, parts):
    out = parts[-1]
    for index in range(len(parts) - 2, -1, -1):
        out = jnp.where(group == index, parts[index], out)
    return out


def packed_inner(product, tiles):
    group = lane_iota(32) // 32
    return by_group(group, [diagonal_sum(product, tile, g) for g, tile in enumerate(tiles)])


def eliminate(packed):
    group = lane_iota(32) // 32
    lane = lane_iota(32)
    row32 = lax.broadcasted_iota(jnp.int32, (32, 128), 0)
    eye = jnp.where(lane == row32 + 96, 1.0, 0.0).astype(F32)
    down = pltpu.roll(packed, 96, 1)
    up = pltpu.roll(packed, 32, 1)
    top = by_group(group, [packed, -packed, packed, eye])
    bottom = by_group(group, [down, up, down, jnp.zeros_like(packed)])
    work = jnp.concatenate([top, bottom], axis=0)
    row = lax.broadcasted_iota(jnp.int32, (64, 128), 0)
    for k in range(RHS):
        inverse = 1.0 / work[k : k + 1, k : k + 1]
        first = work[k : k + 1, :] * inverse
        second = work[k + 32 : k + 33, :] * inverse
        updated = work - work[:, k : k + 1] * first - work[:, k + 32 : k + 33] * second
        work = jnp.where(row == k, first, jnp.where(row == k + 32, second, updated))
    return work


def repeated(block, group_index):
    group = lane_iota(32) // 32
    block = jnp.where(group == group_index, block, 0.0)
    block = block + pltpu.roll(block, 64, 1)
    return block + pltpu.roll(block, 32, 1)


def column_matrix(coef, group_index):
    group = lane_iota(32) // 32
    real = repeated(coef[:32], group_index)
    imag = repeated(coef[32:], group_index)
    blocks = [jnp.where(group == y, real, 0.0) for y in range(NY)]
    blocks += [jnp.where(group == y, -imag, 0.0) for y in range(NY)]
    return jnp.concatenate(blocks, axis=0)


def kernel(
    sizes,
    b_ref,
    self_ref,
    hop_ref,
    sol_ref,
    res_ref,
    raw,
    rows_scr,
    amat,
    bhi,
    blo,
    ext,
    halo,
    acc,
    second,
    pay,
    rs_buf,
    y_buf,
    z_buf,
    ag_buf,
    link_sem,
    b_sem,
    halo_send,
    halo_recv,
    t_send,
    t_recv,
    red_send,
    red_recv,
):
    yb, zb, xb = sizes
    zt = lax.axis_index("zt")
    xy = lax.axis_index("xy")
    my_y = lax.rem(zt, yb)
    my_z = lax.div(zt, yb)
    count = yb * zb

    def zt_at(by):
        return lax.rem(zt + (by + count), count)

    def xy_at(by):
        return lax.rem(xy + (by + xb), xb)

    def link_copies(slot):
        source = self_ref.at[0] if slot == 0 else hop_ref.at[HOP_OF_SLOT[slot], 0]
        return pltpu.make_async_copy(source, raw.at[slot], link_sem.at[slot])

    own = pltpu.make_async_copy(b_ref.at[0], ext.at[0, pl.ds(1, ROWS)], b_sem)
    own.start()
    for slot in range(SLOTS):
        link_copies(slot).start()

    partners = [(zt_at(1), xy), (zt_at(-1), xy)]
    partners += [(my_z * yb + lax.rem(my_y + o, yb), xy) for o in range(1, yb)]
    partners += [(lax.rem(my_z + o, zb) * yb + my_y, xy) for o in range(1, zb)]
    partners += [(zt, lax.rem(xy + o, xb)) for o in range(1, xb)]
    barrier = pltpu.get_barrier_semaphore()
    for partner in partners:
        pl.semaphore_signal(barrier, inc=1, device_id=partner, device_id_type=MESH)
    pl.semaphore_wait(barrier, len(partners))

    targets = ((zt, xy_at(-1)), (zt, xy_at(1)), (zt_at(-yb), xy), (zt_at(yb), xy))

    def halo_copy(which, side, t):
        return pltpu.make_async_remote_copy(
            src_ref=ext.at[which, 1 + t],
            dst_ref=halo.at[which, side, t],
            send_sem=halo_send.at[which, side, t],
            recv_sem=halo_recv.at[which, side, t],
            device_id=targets[side],
            device_id_type=MESH,
        )

    def t_copy(which, side):
        return pltpu.make_async_remote_copy(
            src_ref=ext.at[which, 1 if side == 0 else ROWS],
            dst_ref=ext.at[which, ROWS + 1 if side == 0 else 0],
            send_sem=t_send.at[which, side],
            recv_sem=t_recv.at[which, side],
            device_id=(zt_at(-1) if side == 0 else zt_at(1), xy),
            device_id_type=MESH,
        )

    own.wait()
    t_copy(0, 0).start()
    t_copy(0, 1).start()

    def start_b(t, carry):
        for side in (2, 3, 0, 1):
            halo_copy(0, side, t).start()
        return carry

    lax.fori_loop(0, ROWS, start_b, 0)

    bhi[...] = jnp.zeros_like(bhi)
    blo[...] = jnp.zeros_like(blo)
    for slot in range(SLOTS):
        link_copies(slot).wait()
    lane = lane_iota(8)
    odd = lax.rem(lax.broadcasted_iota(jnp.int32, (8, 128), 0), 2) == 1

    def relayout(step, carry):
        slot = lax.div(step, 2)
        pair = lax.rem(step, 2)
        for g in range(12):
            tiles = [
                raw[slot, pl.ds(2 * pair, 2), :, 384 * g + 128 * n : 384 * g + 128 * (n + 1)].reshape(8, 128)
                for n in range(3)
            ]
            turned = [pltpu.roll(tile, 64, 1) for tile in tiles]
            tiles = [
                jnp.where(odd, jnp.where(lane < 64, turned[n - 1], turned[n]), tiles[n]) for n in range(3)
            ]
            for r in range(8):
                n, offset = divmod(48 * r, 128)
                piece = tiles[n]
                if offset:
                    piece = jnp.where(lane < offset, tiles[(n + 1) % 3], piece)
                    piece = pltpu.roll(piece, 128 - offset, 1)
                rows_scr[pl.ds(8 * g + r, 8, stride=PITCH), :] = piece
        low = lane_iota(96) < 64
        for t in range(2):
            for h in range(2):
                base = (t * 4 + 2 * h) * PITCH
                values = jnp.where(low, rows_scr[base : base + 96, :], rows_scr[base + PITCH : base + PITCH + 96, :])
                hi = values.astype(BF16)
                lo = (values - hi.astype(F32)).astype(BF16)
                amat[2 * pair + t, slot, 0:96, 128 * h : 128 * (h + 1)] = hi
                amat[2 * pair + t, slot, 96:192, 128 * h : 128 * (h + 1)] = lo
        return carry

    lax.fori_loop(0, 2 * SLOTS, relayout, 0)

    group48 = lane_iota(48) // 32

    def put(slot, real, imag):
        for half, part in ((0, real), (1, imag)):
            hi = part.astype(BF16).astype(F32)
            lo = part - hi
            for y in range(NY):
                mask = group48 == y
                at = slice(slot * KSLOT + 64 * y, slot * KSLOT + 64 * y + 48)
                lanes = slice(128 * half, 128 * (half + 1))
                bhi[at, lanes] = jnp.where(mask, hi, 0.0).astype(BF16)
                blo[at, lanes] = jnp.where(mask, lo, 0.0).astype(BF16)

    def put_site(slot, site):
        put(slot, site[0:NV], site[NV : 2 * NV])

    def product(t, first, last):
        left = jnp.concatenate([amat[t, s] for s in range(first, last)], axis=1)
        right = slice(first * KSLOT, last * KSLOT)
        main = jnp.dot(left, bhi[right, :], preferred_element_type=F32)
        rest = jnp.dot(left[0:96], blo[right, :], preferred_element_type=F32)
        return main[0:96] + main[96:192] + rest

    def near_sites(site):
        put_site(0, -site)
        put_site(1, pltpu.roll(site, 96, 1))
        put_site(2, pltpu.roll(site, 32, 1))

    def near(which):
        def body(t, carry):
            site = ext[which, 1 + t]
            near_sites(site)
            acc[t] = product(t, 0, 3)
            return carry

        lax.fori_loop(0, ROWS, body, 0)

    def far(which, out):
        t_copy(which, 0).wait_recv()
        t_copy(which, 1).wait_recv()

        def body(t, carry):
            for side in range(4):
                halo_copy(which, side, t).wait_recv()
            put_site(3, ext[which, 2 + t])
            put_site(4, ext[which, t])
            for side in range(4):
                put_site(5 + side, halo[which, side, t])
            if which:
                total = acc[t] + product(t, 3, SLOTS)
            else:
                near_sites(ext[which, 1 + t])
                total = product(t, 0, SLOTS)
            real = total[48:96, 128:256] - total[0:48, 0:128]
            imag = -(total[48:96, 0:128] + total[0:48, 128:256])
            out(t, real, imag)
            return carry

        lax.fori_loop(0, ROWS, body, 0)

    def image_out(t, real, imag):
        ext[1, 1 + t, 0:NV, :] = real
        ext[1, 1 + t, NV : 2 * NV, :] = imag
        for side in (2, 3, 0, 1):
            halo_copy(1, side, t).start()

    far(0, image_out)
    t_copy(1, 0).start()
    t_copy(1, 1).start()

    piece = 64 // xb

    def exchange(red, phase, buffer, me, size, source, device):
        def copy(o):
            return pltpu.make_async_remote_copy(
                src_ref=source(lax.rem(me + o, size)),
                dst_ref=buffer.at[red, me],
                send_sem=red_send.at[red, phase, o],
                recv_sem=red_recv.at[red, phase, me],
                device_id=device(lax.rem(me + o, size)),
                device_id_type=MESH,
            )

        def arrival(o):
            other = lax.rem(me + o, size)
            return pltpu.make_async_remote_copy(
                src_ref=source(other),
                dst_ref=buffer.at[red, other],
                send_sem=red_send.at[red, phase, o],
                recv_sem=red_recv.at[red, phase, other],
                device_id=device(other),
                device_id_type=MESH,
            )

        def start():
            for o in range(1, size):
                copy(o).start()

        def wait():
            for o in range(1, size):
                arrival(o).wait_recv()

        def drain():
            for o in range(1, size):
                copy(o).wait_send()

        return start, wait, drain

    def y_device(other):
        return (my_z * yb + other, xy)

    def z_device(other):
        return (other * yb + my_y, xy)

    def x_device(other):
        return (zt, other)

    def reduction(red):
        scatter = exchange(red, 0, rs_buf, xy, xb, lambda other: pay.at[red, other], x_device)
        along_y = exchange(red, 1, y_buf, my_y, yb, lambda other: y_buf.at[red, my_y], y_device)
        along_z = exchange(red, 2, z_buf, my_z, zb, lambda other: z_buf.at[red, my_z], z_device)
        gather = exchange(red, 3, ag_buf, xy, xb, lambda other: ag_buf.at[red, xy], x_device)

        def summed(buffer, size):
            total = buffer[red, 0]
            for n in range(1, size):
                total = total + buffer[red, n]
            return total

        def step0(values):
            for n in range(xb):
                pay[red, n] = values[n * piece : (n + 1) * piece]
            rs_buf[red, xy] = pay[red, xy]
            scatter[0]()

        def step1():
            scatter[1]()
            y_buf[red, my_y] = summed(rs_buf, xb)
            along_y[0]()

        def step2():
            along_y[1]()
            z_buf[red, my_z] = summed(y_buf, yb)
            along_z[0]()

        def step3():
            along_z[1]()
            ag_buf[red, xy] = summed(z_buf, zb)
            gather[0]()

        def step4():
            gather[1]()
            return jnp.concatenate([ag_buf[red, n] for n in range(xb)], axis=0)

        def drain():
            for part in (scatter, along_y, along_z, gather):
                part[2]()

        return step0, step1, step2, step3, step4, drain

    red1 = reduction(0)
    red2 = reduction(1)
    group = lane_iota(32) // 32
    group64 = lane_iota(64) // 32
    zero32 = jnp.zeros((32, 128), F32)

    rhs_rows = field_rows(ext.at[0], 1)
    rhs_pair = jnp.concatenate([rhs_rows, field_j(rhs_rows)], axis=1)
    image_rows = field_rows(ext.at[1], 1)
    image_pair = jnp.concatenate([image_rows, field_j(image_rows)], axis=1)
    inner = dot(image_rows.T, jnp.concatenate([image_pair, rhs_pair], axis=1))
    packed = packed_inner(inner, (0, 1, 2, 3))
    red1[0](jnp.concatenate([packed, zero32], axis=0))

    near(1)
    red1[1]()

    def twice_out(t, real, imag):
        second[t, 0:NV, :] = real
        second[t, NV : 2 * NV, :] = imag

    far(1, twice_out)

    rhs_rows = field_rows(ext.at[0], 1)
    rhs_pair = jnp.concatenate([rhs_rows, field_j(rhs_rows)], axis=1)
    image_rows = field_rows(ext.at[1], 1)
    image_pair = jnp.concatenate([image_rows, field_j(image_rows)], axis=1)
    twice_rows = field_rows(second)
    twice_pair = jnp.concatenate([twice_rows, field_j(twice_rows)], axis=1)
    with_image = dot(image_rows.T, twice_pair)
    with_twice = dot(twice_rows.T, jnp.concatenate([image_pair, twice_pair, rhs_pair], axis=1))
    with_both = jnp.concatenate([with_image, with_twice[:, 0:256]], axis=1)
    red2[0](
        jnp.concatenate(
            [packed_inner(with_both, (0, 1, 2, 3)), packed_inner(with_twice, (2, 3, 4, 5))], axis=0
        )
    )

    def real_form(real, imag):
        top = by_group(group, [real, -pltpu.roll(imag, 32, 1), zero32, zero32])
        bottom = by_group(group, [imag, pltpu.roll(real, 32, 1), zero32, zero32])
        return jnp.concatenate([top, bottom], axis=0)

    def stacked(packed, first):
        turns = [pltpu.roll(packed, (128 - 32 * g) % 128, 1) if g else packed for g in (first, first + 1)]
        return jnp.where(group64 == 0, jnp.concatenate(turns, axis=0), 0.0)

    def form_of(column):
        return real_form(column[:32], column[32:])

    red1[2]()
    red2[1]()
    red1[3]()
    red2[2]()
    gram = red1[4]()[0:32]
    solved = eliminate(gram)
    gram_column = stacked(gram, 0)
    gram_form = form_of(gram_column)
    target_column = stacked(gram, 2)
    coef1 = jnp.where(group64 == 0, pltpu.roll(solved, 64, 1), 0.0)
    inverse_form = form_of(pltpu.roll(solved, 32, 1))
    coef1_form = form_of(coef1)
    red2[3]()
    reduced = red2[4]()
    upper, lower = reduced[:32], reduced[32:]

    cross_form = form_of(stacked(upper, 0))
    image_part = gram_column - dot(cross_form[:, 0:64], coef1)
    projection = dot(inverse_form[:, 0:64], image_part)
    row64 = lax.broadcasted_iota(jnp.int32, (64, 128), 0)
    identity = jnp.where(lane_iota(64) == row64, jnp.where(group64 == 0, 1.0, 0.0), 0.0).astype(F32)
    keep = identity - projection

    grams = jnp.concatenate(
        [
            gram_form + pltpu.roll(cross_form, 64, 1),
            form_of(stacked(upper, 2)) + pltpu.roll(form_of(stacked(lower, 0)), 64, 1),
        ],
        axis=0,
    )
    weights = jnp.concatenate([keep, -coef1], axis=0)
    applied = dot(grams, weights - jnp.concatenate([pltpu.roll(coef1, 64, 1), jnp.zeros_like(coef1)], axis=0))
    targets12 = jnp.concatenate([target_column, stacked(lower, 2)], axis=0)
    applied = applied + pltpu.roll(targets12, 64, 1)
    turned = jnp.concatenate([times_minus_i(applied[:64]), times_minus_i(applied[64:])], axis=0)
    applied = applied + pltpu.roll(turned, 32, 1)
    solved2 = eliminate(dot(weights.T, applied)[0:32])

    follow = dot(jnp.concatenate([form_of(keep), coef1_form], axis=0)[:, 0:64], solved2)
    step_a = column_matrix(pltpu.roll(coef1, 64, 1) + follow[:64], 2)
    step_e = column_matrix(follow[64:], 2)
    rhs_rows = field_rows(ext.at[0], 1)
    rhs_pair = jnp.concatenate([rhs_rows, field_j(rhs_rows)], axis=1)
    image_rows = field_rows(ext.at[1], 1)
    image_pair = jnp.concatenate([image_rows, field_j(image_rows)], axis=1)
    twice_rows = field_rows(second)
    twice_pair = jnp.concatenate([twice_rows, field_j(twice_rows)], axis=1)
    answer = dot(jnp.concatenate([rhs_pair, image_pair], axis=1), jnp.concatenate([step_a, -step_e], axis=0))
    sol_ref[0] = answer.reshape(ROWS, 2 * NV, 128)
    change = dot(jnp.concatenate([image_pair, twice_pair], axis=1), jnp.concatenate([-step_a, step_e], axis=0))
    res_ref[0] = (rhs_rows + change).reshape(ROWS, 2 * NV, 128)

    for which in range(2):
        t_copy(which, 0).wait_send()
        t_copy(which, 1).wait_send()

    def drain(t, carry):
        for which in range(2):
            for side in range(4):
                halo_copy(which, side, t).wait_send()
        return carry

    lax.fori_loop(0, ROWS, drain, 0)
    red1[5]()
    red2[5]()


def solution(mesh):
    yb = NT // ROWS
    zb = mesh.shape["zt"] // yb
    xb = mesh.shape["xy"]
    piece = 64 // xb
    block = jax.ShapeDtypeStruct((1, ROWS, 2 * NV, 128), F32)

    def local(right_side, self_link, hop_links):
        in_hbm = pl.BlockSpec(memory_space=pltpu.HBM)
        in_vmem = pl.BlockSpec(memory_space=pltpu.VMEM)
        return pl.pallas_call(
            functools.partial(kernel, (yb, zb, xb)),
            out_shape=(block, block),
            in_specs=[in_hbm, in_hbm, in_hbm],
            out_specs=(in_vmem, in_vmem),
            scratch_shapes=[
                pltpu.VMEM((SLOTS, ROWS, NY, 2 * NV * NV), F32),
                pltpu.VMEM((8 * PITCH, 128), F32),
                pltpu.VMEM((ROWS, SLOTS, 192, KSLOT), BF16),
                pltpu.VMEM((SLOTS * KSLOT, 256), BF16),
                pltpu.VMEM((SLOTS * KSLOT, 256), BF16),
                pltpu.VMEM((2, ROWS + 2, 2 * NV, 128), F32),
                pltpu.VMEM((2, 4, ROWS, 2 * NV, 128), F32),
                pltpu.VMEM((ROWS, 96, 256), F32),
                pltpu.VMEM((ROWS, 2 * NV, 128), F32),
                pltpu.VMEM((2, xb, piece, 128), F32),
                pltpu.VMEM((2, xb, piece, 128), F32),
                pltpu.VMEM((2, yb, piece, 128), F32),
                pltpu.VMEM((2, zb, piece, 128), F32),
                pltpu.VMEM((2, xb, piece, 128), F32),
                pltpu.SemaphoreType.DMA((SLOTS,)),
                pltpu.SemaphoreType.DMA,
                pltpu.SemaphoreType.DMA((2, 4, ROWS)),
                pltpu.SemaphoreType.DMA((2, 4, ROWS)),
                pltpu.SemaphoreType.DMA((2, 2)),
                pltpu.SemaphoreType.DMA((2, 2)),
                pltpu.SemaphoreType.DMA((2, 4, 8)),
                pltpu.SemaphoreType.DMA((2, 4, 8)),
            ],
            compiler_params=pltpu.CompilerParams(
                collective_id=0, has_side_effects=True, vmem_limit_bytes=48 * 1024 * 1024
            ),
            name="two_gcr_iterations",
        )(*[pltpu.with_memory_space_constraint(x, pltpu.HBM) for x in (right_side, self_link, hop_links)])

    return jax.shard_map(
        local,
        mesh=mesh,
        in_specs=(
            P("xy", "zt", None, None),
            P("xy", "zt", None, None),
            P(None, "xy", "zt", None, None),
        ),
        out_specs=(P("xy", "zt", None, None), P("xy", "zt", None, None)),
        check_vma=False,
    )
```

```python
import functools

import jax
import jax.numpy as jnp
from jax import lax
from jax.experimental import pallas as pl
from jax.experimental.pallas import tpu as pltpu
from jax.sharding import PartitionSpec as P

NV = 48
RHS = 32
NT = 32
NY = 4
ROWS = 4

MESH = pl.DeviceIdType.MESH
HIGHEST = lax.Precision.HIGHEST
F32 = jnp.float32
BF16 = jnp.bfloat16

HOP_OF_SLOT = (None, 2, 3, 6, 7, 0, 1, 4, 5)
SLOTS = 9
KSLOT = 256
PITCH = 97


def dot(left, right):
    return jnp.dot(left, right, precision=HIGHEST, preferred_element_type=F32)


def lane_iota(rows):
    return lax.broadcasted_iota(jnp.int32, (rows, 128), 1)


def times_minus_i(rows):
    half = rows.shape[0] // 2
    return jnp.concatenate([rows[half:], -rows[:half]], axis=0)


def field_rows(ref, first=0):
    return ref[first : first + ROWS].reshape(ROWS * 2 * NV, 128)


def field_j(rows):
    parts = []
    for t in range(ROWS):
        base = t * 2 * NV
        parts.append(rows[base + NV : base + 2 * NV])
        parts.append(-rows[base : base + NV])
    return jnp.concatenate(parts, axis=0)


def diagonal_sum(product, tile, group):
    total = None
    for y in range(NY):
        block = product[32 * y : 32 * (y + 1), 128 * tile : 128 * (tile + 1)]
        shift = (32 * (group - y)) % 128
        if shift:
            block = pltpu.roll(block, shift, 1)
        total = block if total is None else total + block
    return total


def by_group(group, parts):
    out = parts[-1]
    for index in range(len(parts) - 2, -1, -1):
        out = jnp.where(group == index, parts[index], out)
    return out


def packed_inner(product, tiles):
    group = lane_iota(32) // 32
    return by_group(group, [diagonal_sum(product, tile, g) for g, tile in enumerate(tiles)])


def eliminate(packed):
    group = lane_iota(32) // 32
    lane = lane_iota(32)
    row32 = lax.broadcasted_iota(jnp.int32, (32, 128), 0)
    eye = jnp.where(lane == row32 + 96, 1.0, 0.0).astype(F32)
    down = pltpu.roll(packed, 96, 1)
    up = pltpu.roll(packed, 32, 1)
    top = by_group(group, [packed, -packed, packed, eye])
    bottom = by_group(group, [down, up, down, jnp.zeros_like(packed)])
    work = jnp.concatenate([top, bottom], axis=0)
    row = lax.broadcasted_iota(jnp.int32, (64, 128), 0)

    def whole(value):
        return jnp.broadcast_to(value, (8, 128))

    for k in range(0, RHS, 2):
        n = k + 1

        def at(i, j):
            return whole(work[i : i + 1, j : j + 1])

        inverse = 1.0 / at(k, k)
        first1 = whole(work[k : k + 1, :]) * inverse
        first2 = whole(work[k + 32 : k + 33, :]) * inverse
        col1, col2 = work[:, k : k + 1], work[:, k + 32 : k + 33]
        next1 = whole(work[n : n + 1, :]) - at(n, k) * first1 - at(n, k + 32) * first2
        next2 = whole(work[n + 32 : n + 33, :]) - at(n + 32, k) * first1 - at(n + 32, k + 32) * first2
        drop = at(n, k) * at(k, n) + at(n, k + 32) * at(k + 32, n)
        inverse2 = 1.0 / (at(n, n) - drop * inverse)
        second1, second2 = next1 * inverse2, next2 * inverse2
        up11, up21 = at(k, n) * inverse, at(k + 32, n) * inverse
        up12, up22 = at(k, n + 32) * inverse, at(k + 32, n + 32) * inverse
        later1 = work[:, n : n + 1] - col1 * up11[0:1] - col2 * up21[0:1]
        later2 = work[:, n + 32 : n + 33] - col1 * up12[0:1] - col2 * up22[0:1]
        updated = work - col1 * first1[0:1] - col2 * first2[0:1] - later1 * second1[0:1] - later2 * second2[0:1]
        first1, first2 = (
            first1 - up11 * second1 - up12 * second2,
            first2 - up21 * second1 - up22 * second2,
        )
        for place, value in ((k, first1), (k + 32, first2), (n, second1), (n + 32, second2)):
            updated = jnp.where(row == place, value[0:1], updated)
        work = updated
    return work


def repeated(block, group_index):
    group = lane_iota(32) // 32
    block = jnp.where(group == group_index, block, 0.0)
    block = block + pltpu.roll(block, 64, 1)
    return block + pltpu.roll(block, 32, 1)


def column_matrix(coef, group_index):
    group = lane_iota(32) // 32
    real = repeated(coef[:32], group_index)
    imag = repeated(coef[32:], group_index)
    blocks = [jnp.where(group == y, real, 0.0) for y in range(NY)]
    blocks += [jnp.where(group == y, -imag, 0.0) for y in range(NY)]
    return jnp.concatenate(blocks, axis=0)


def kernel(
    sizes,
    b_ref,
    self_ref,
    hop_ref,
    sol_ref,
    res_ref,
    raw,
    rows_scr,
    amat,
    bhi,
    blo,
    ext,
    halo,
    acc,
    second,
    pieces,
    pay,
    rs_buf,
    y_buf,
    z_buf,
    ag_buf,
    link_sem,
    b_sem,
    halo_send,
    halo_recv,
    t_send,
    t_recv,
    red_send,
    red_recv,
):
    yb, zb, xb = sizes
    zt = lax.axis_index("zt")
    xy = lax.axis_index("xy")
    my_y = lax.rem(zt, yb)
    my_z = lax.div(zt, yb)
    count = yb * zb

    def zt_at(by):
        return lax.rem(zt + (by + count), count)

    def xy_at(by):
        return lax.rem(xy + (by + xb), xb)

    def link_copies(slot):
        source = self_ref.at[0] if slot == 0 else hop_ref.at[HOP_OF_SLOT[slot], 0]
        return pltpu.make_async_copy(source, raw.at[slot], link_sem.at[slot])

    own = pltpu.make_async_copy(b_ref.at[0], ext.at[0, pl.ds(1, ROWS)], b_sem)
    own.start()
    for slot in range(SLOTS):
        link_copies(slot).start()

    partners = [(zt_at(1), xy), (zt_at(-1), xy)]
    partners += [(my_z * yb + lax.rem(my_y + o, yb), xy) for o in range(1, yb)]
    partners += [(lax.rem(my_z + o, zb) * yb + my_y, xy) for o in range(1, zb)]
    partners += [(zt, lax.rem(xy + o, xb)) for o in range(1, xb)]
    barrier = pltpu.get_barrier_semaphore()
    for partner in partners:
        pl.semaphore_signal(barrier, inc=1, device_id=partner, device_id_type=MESH)
    pl.semaphore_wait(barrier, len(partners))

    targets = ((zt, xy_at(-1)), (zt, xy_at(1)), (zt_at(-yb), xy), (zt_at(yb), xy))

    def halo_copy(which, side, t):
        return pltpu.make_async_remote_copy(
            src_ref=ext.at[which, 1 + t],
            dst_ref=halo.at[which, side, t],
            send_sem=halo_send.at[which, side, t],
            recv_sem=halo_recv.at[which, side, t],
            device_id=targets[side],
            device_id_type=MESH,
        )

    def t_copy(which, side):
        return pltpu.make_async_remote_copy(
            src_ref=ext.at[which, 1 if side == 0 else ROWS],
            dst_ref=ext.at[which, ROWS + 1 if side == 0 else 0],
            send_sem=t_send.at[which, side],
            recv_sem=t_recv.at[which, side],
            device_id=(zt_at(-1) if side == 0 else zt_at(1), xy),
            device_id_type=MESH,
        )

    own.wait()
    t_copy(0, 0).start()
    t_copy(0, 1).start()

    def start_b(t, carry):
        for side in (2, 3, 0, 1):
            halo_copy(0, side, t).start()
        return carry

    lax.fori_loop(0, ROWS, start_b, 0)

    bhi[...] = jnp.zeros_like(bhi)
    blo[...] = jnp.zeros_like(blo)
    for slot in range(SLOTS):
        link_copies(slot).wait()
    lane = lane_iota(8)
    odd = lax.rem(lax.broadcasted_iota(jnp.int32, (8, 128), 0), 2) == 1

    def relayout(step, carry):
        slot = lax.div(step, 2)
        pair = lax.rem(step, 2)
        for g in range(12):
            tiles = [
                raw[slot, pl.ds(2 * pair, 2), :, 384 * g + 128 * n : 384 * g + 128 * (n + 1)].reshape(8, 128)
                for n in range(3)
            ]
            turned = [pltpu.roll(tile, 64, 1) for tile in tiles]
            tiles = [
                jnp.where(odd, jnp.where(lane < 64, turned[n - 1], turned[n]), tiles[n]) for n in range(3)
            ]
            for r in range(8):
                n, offset = divmod(48 * r, 128)
                piece = tiles[n]
                if offset:
                    piece = jnp.where(lane < offset, tiles[(n + 1) % 3], piece)
                    piece = pltpu.roll(piece, 128 - offset, 1)
                rows_scr[pl.ds(8 * g + r, 8, stride=PITCH), :] = piece
        low = lane_iota(96) < 64
        for t in range(2):
            for h in range(2):
                base = (t * 4 + 2 * h) * PITCH
                values = jnp.where(low, rows_scr[base : base + 96, :], rows_scr[base + PITCH : base + PITCH + 96, :])
                hi = values.astype(BF16)
                lo = (values - hi.astype(F32)).astype(BF16)
                amat[2 * pair + t, slot, 0:96, 128 * h : 128 * (h + 1)] = hi
                amat[2 * pair + t, slot, 96:192, 128 * h : 128 * (h + 1)] = lo
        return carry

    lax.fori_loop(0, 2 * SLOTS, relayout, 0)

    group48 = lane_iota(48) // 32

    def put(slot, real, imag):
        for half, part in ((0, real), (1, imag)):
            hi = part.astype(BF16).astype(F32)
            lo = part - hi
            for y in range(NY):
                mask = group48 == y
                at = slice(slot * KSLOT + 64 * y, slot * KSLOT + 64 * y + 48)
                lanes = slice(128 * half, 128 * (half + 1))
                bhi[at, lanes] = jnp.where(mask, hi, 0.0).astype(BF16)
                blo[at, lanes] = jnp.where(mask, lo, 0.0).astype(BF16)

    def put_site(slot, site):
        put(slot, site[0:NV], site[NV : 2 * NV])

    def product(t, first, last):
        left = jnp.concatenate([amat[t, s] for s in range(first, last)], axis=1)
        right = slice(first * KSLOT, last * KSLOT)
        main = jnp.dot(left, bhi[right, :], preferred_element_type=F32)
        rest = jnp.dot(left[0:96], blo[right, :], preferred_element_type=F32)
        return main[0:96] + main[96:192] + rest

    def near_sites(site):
        put_site(0, -site)
        put_site(1, pltpu.roll(site, 96, 1))
        put_site(2, pltpu.roll(site, 32, 1))

    def near(which):
        def body(t, carry):
            site = ext[which, 1 + t]
            near_sites(site)
            acc[t] = product(t, 0, 3)
            return carry

        lax.fori_loop(0, ROWS, body, 0)

    def far(which, out):
        t_copy(which, 0).wait_recv()
        t_copy(which, 1).wait_recv()

        def body(t, carry):
            for side in range(4):
                halo_copy(which, side, t).wait_recv()
            put_site(3, ext[which, 2 + t])
            put_site(4, ext[which, t])
            for side in range(4):
                put_site(5 + side, halo[which, side, t])
            if which:
                total = acc[t] + product(t, 3, SLOTS)
            else:
                near_sites(ext[which, 1 + t])
                total = product(t, 0, SLOTS)
            real = total[48:96, 128:256] - total[0:48, 0:128]
            imag = -(total[48:96, 0:128] + total[0:48, 128:256])
            out(t, real, imag)
            return carry

        lax.fori_loop(0, ROWS, body, 0)

    def image_out(t, real, imag):
        ext[1, 1 + t, 0:NV, :] = real
        ext[1, 1 + t, NV : 2 * NV, :] = imag
        for side in (2, 3, 0, 1):
            halo_copy(1, side, t).start()

    far(0, image_out)
    t_copy(1, 0).start()
    t_copy(1, 1).start()

    piece = 64 // xb

    def exchange(red, phase, buffer, me, size, source, device):
        def copy(o):
            return pltpu.make_async_remote_copy(
                src_ref=source(lax.rem(me + o, size)),
                dst_ref=buffer.at[red, me],
                send_sem=red_send.at[red, phase, o],
                recv_sem=red_recv.at[red, phase, me],
                device_id=device(lax.rem(me + o, size)),
                device_id_type=MESH,
            )

        def arrival(o):
            other = lax.rem(me + o, size)
            return pltpu.make_async_remote_copy(
                src_ref=source(other),
                dst_ref=buffer.at[red, other],
                send_sem=red_send.at[red, phase, o],
                recv_sem=red_recv.at[red, phase, other],
                device_id=device(other),
                device_id_type=MESH,
            )

        def start():
            for o in range(1, size):
                copy(o).start()

        def wait():
            for o in range(1, size):
                arrival(o).wait_recv()

        def drain():
            for o in range(1, size):
                copy(o).wait_send()

        return start, wait, drain

    def y_device(other):
        return (my_z * yb + other, xy)

    def z_device(other):
        return (other * yb + my_y, xy)

    def x_device(other):
        return (zt, other)

    def reduction(red):
        scatter = exchange(red, 0, rs_buf, xy, xb, lambda other: pay.at[red, other], x_device)
        along_y = exchange(red, 1, y_buf, my_y, yb, lambda other: y_buf.at[red, my_y], y_device)
        along_z = exchange(red, 2, z_buf, my_z, zb, lambda other: z_buf.at[red, my_z], z_device)
        gather = exchange(red, 3, ag_buf, xy, xb, lambda other: ag_buf.at[red, xy], x_device)

        def summed(buffer, size):
            total = buffer[red, 0]
            for n in range(1, size):
                total = total + buffer[red, n]
            return total

        def step0(values):
            for n in range(xb):
                pay[red, n] = values[n * piece : (n + 1) * piece]
            rs_buf[red, xy] = pay[red, xy]
            scatter[0]()

        def step1():
            scatter[1]()
            y_buf[red, my_y] = summed(rs_buf, xb)
            along_y[0]()

        def step2():
            along_y[1]()
            z_buf[red, my_z] = summed(y_buf, yb)
            along_z[0]()

        def step3():
            along_z[1]()
            ag_buf[red, xy] = summed(z_buf, zb)
            gather[0]()

        def step4():
            gather[1]()
            return jnp.concatenate([ag_buf[red, n] for n in range(xb)], axis=0)

        def drain():
            for part in (scatter, along_y, along_z, gather):
                part[2]()

        return step0, step1, step2, step3, step4, drain

    red1 = reduction(0)
    red2 = reduction(1)
    group = lane_iota(32) // 32
    group64 = lane_iota(64) // 32
    zero32 = jnp.zeros((32, 128), F32)

    rhs_rows = field_rows(ext.at[0], 1)
    rhs_pair = jnp.concatenate([rhs_rows, field_j(rhs_rows)], axis=1)
    image_rows = field_rows(ext.at[1], 1)
    image_pair = jnp.concatenate([image_rows, field_j(image_rows)], axis=1)
    inner = dot(image_rows.T, jnp.concatenate([image_pair, rhs_pair], axis=1))
    packed = packed_inner(inner, (0, 1, 2, 3))
    red1[0](jnp.concatenate([packed, zero32], axis=0))

    near(1)
    red1[1]()

    def twice_out(t, real, imag):
        second[t, 0:NV, :] = real
        second[t, NV : 2 * NV, :] = imag

    far(1, twice_out)

    rhs_rows = field_rows(ext.at[0], 1)
    rhs_pair = jnp.concatenate([rhs_rows, field_j(rhs_rows)], axis=1)
    image_rows = field_rows(ext.at[1], 1)
    image_pair = jnp.concatenate([image_rows, field_j(image_rows)], axis=1)
    twice_rows = field_rows(second)
    twice_pair = jnp.concatenate([twice_rows, field_j(twice_rows)], axis=1)
    with_image = dot(image_rows.T, twice_pair)
    with_twice = dot(twice_rows.T, jnp.concatenate([image_pair, twice_pair, rhs_pair], axis=1))
    with_both = jnp.concatenate([with_image, with_twice[:, 0:256]], axis=1)
    red2[0](
        jnp.concatenate(
            [packed_inner(with_both, (0, 1, 2, 3)), packed_inner(with_twice, (2, 3, 4, 5))], axis=0
        )
    )

    def real_form(real, imag):
        top = by_group(group, [real, -pltpu.roll(imag, 32, 1), zero32, zero32])
        bottom = by_group(group, [imag, pltpu.roll(real, 32, 1), zero32, zero32])
        return jnp.concatenate([top, bottom], axis=0)

    def stacked(packed, first):
        turns = [pltpu.roll(packed, (128 - 32 * g) % 128, 1) if g else packed for g in (first, first + 1)]
        return jnp.where(group64 == 0, jnp.concatenate(turns, axis=0), 0.0)

    def form_of(column):
        return real_form(column[:32], column[32:])

    def split(values):
        hi = values.astype(BF16)
        return hi, (values - hi.astype(F32)).astype(BF16)

    def keep_pieces(index, ref, first):
        rows = field_rows(ref, first)
        hi, lo = split(jnp.concatenate([rows, field_j(rows)], axis=1))
        pieces[index, 0] = hi
        pieces[index, 1] = lo

    def combined(index, coef):
        hi, lo = split(coef)
        field_hi = pieces[index, 0]
        out = jnp.dot(field_hi, hi, preferred_element_type=F32)
        out = out + jnp.dot(pieces[index, 1], hi, preferred_element_type=F32)
        return out + jnp.dot(field_hi, lo, preferred_element_type=F32)

    red1[2]()
    red2[1]()
    keep_pieces(0, ext.at[0], 1)
    keep_pieces(1, ext.at[1], 1)
    keep_pieces(2, second, 0)
    red1[3]()
    red2[2]()
    gram = red1[4]()[0:32]
    solved = eliminate(gram)
    gram_column = stacked(gram, 0)
    gram_form = form_of(gram_column)
    target_column = stacked(gram, 2)
    coef1 = jnp.where(group64 == 0, pltpu.roll(solved, 64, 1), 0.0)
    inverse_form = form_of(pltpu.roll(solved, 32, 1))
    coef1_form = form_of(coef1)
    red2[3]()
    reduced = red2[4]()
    upper, lower = reduced[:32], reduced[32:]

    cross_form = form_of(stacked(upper, 0))
    image_part = gram_column - dot(cross_form[:, 0:64], coef1)
    projection = dot(inverse_form[:, 0:64], image_part)
    row64 = lax.broadcasted_iota(jnp.int32, (64, 128), 0)
    identity = jnp.where(lane_iota(64) == row64, jnp.where(group64 == 0, 1.0, 0.0), 0.0).astype(F32)
    keep = identity - projection

    grams = jnp.concatenate(
        [
            gram_form + pltpu.roll(cross_form, 64, 1),
            form_of(stacked(upper, 2)) + pltpu.roll(form_of(stacked(lower, 0)), 64, 1),
        ],
        axis=0,
    )
    weights = jnp.concatenate([keep, -coef1], axis=0)
    applied = dot(grams, weights - jnp.concatenate([pltpu.roll(coef1, 64, 1), jnp.zeros_like(coef1)], axis=0))
    targets12 = jnp.concatenate([target_column, stacked(lower, 2)], axis=0)
    applied = applied + pltpu.roll(targets12, 64, 1)
    turned = jnp.concatenate([times_minus_i(applied[:64]), times_minus_i(applied[64:])], axis=0)
    applied = applied + pltpu.roll(turned, 32, 1)
    solved2 = eliminate(dot(weights.T, applied)[0:32])

    follow = dot(jnp.concatenate([form_of(keep), coef1_form], axis=0)[:, 0:64], solved2)
    step_a = column_matrix(pltpu.roll(coef1, 64, 1) + follow[:64], 2)
    step_e = column_matrix(follow[64:], 2)
    from_image = combined(1, jnp.concatenate([-step_e, -step_a], axis=1))
    sol_ref[0] = (combined(0, step_a) + from_image[:, 0:128]).reshape(ROWS, 2 * NV, 128)
    change = combined(2, step_e) + from_image[:, 128:256]
    res_ref[0] = (field_rows(ext.at[0], 1) + change).reshape(ROWS, 2 * NV, 128)

    for which in range(2):
        t_copy(which, 0).wait_send()
        t_copy(which, 1).wait_send()

    def drain(t, carry):
        for which in range(2):
            for side in range(4):
                halo_copy(which, side, t).wait_send()
        return carry

    lax.fori_loop(0, ROWS, drain, 0)
    red1[5]()
    red2[5]()


def solution(mesh):
    yb = NT // ROWS
    zb = mesh.shape["zt"] // yb
    xb = mesh.shape["xy"]
    piece = 64 // xb
    block = jax.ShapeDtypeStruct((1, ROWS, 2 * NV, 128), F32)

    def local(right_side, self_link, hop_links):
        in_hbm = pl.BlockSpec(memory_space=pltpu.HBM)
        in_vmem = pl.BlockSpec(memory_space=pltpu.VMEM)
        return pl.pallas_call(
            functools.partial(kernel, (yb, zb, xb)),
            out_shape=(block, block),
            in_specs=[in_hbm, in_hbm, in_hbm],
            out_specs=(in_vmem, in_vmem),
            scratch_shapes=[
                pltpu.VMEM((SLOTS, ROWS, NY, 2 * NV * NV), F32),
                pltpu.VMEM((8 * PITCH, 128), F32),
                pltpu.VMEM((ROWS, SLOTS, 192, KSLOT), BF16),
                pltpu.VMEM((SLOTS * KSLOT, 256), BF16),
                pltpu.VMEM((SLOTS * KSLOT, 256), BF16),
                pltpu.VMEM((2, ROWS + 2, 2 * NV, 128), F32),
                pltpu.VMEM((2, 4, ROWS, 2 * NV, 128), F32),
                pltpu.VMEM((ROWS, 96, 256), F32),
                pltpu.VMEM((ROWS, 2 * NV, 128), F32),
                pltpu.VMEM((3, 2, ROWS * 2 * NV, 256), BF16),
                pltpu.VMEM((2, xb, piece, 128), F32),
                pltpu.VMEM((2, xb, piece, 128), F32),
                pltpu.VMEM((2, yb, piece, 128), F32),
                pltpu.VMEM((2, zb, piece, 128), F32),
                pltpu.VMEM((2, xb, piece, 128), F32),
                pltpu.SemaphoreType.DMA((SLOTS,)),
                pltpu.SemaphoreType.DMA,
                pltpu.SemaphoreType.DMA((2, 4, ROWS)),
                pltpu.SemaphoreType.DMA((2, 4, ROWS)),
                pltpu.SemaphoreType.DMA((2, 2)),
                pltpu.SemaphoreType.DMA((2, 2)),
                pltpu.SemaphoreType.DMA((2, 4, 8)),
                pltpu.SemaphoreType.DMA((2, 4, 8)),
            ],
            compiler_params=pltpu.CompilerParams(
                collective_id=0, has_side_effects=True, vmem_limit_bytes=48 * 1024 * 1024
            ),
            name="two_gcr_iterations",
        )(*[pltpu.with_memory_space_constraint(x, pltpu.HBM) for x in (right_side, self_link, hop_links)])

    return jax.shard_map(
        local,
        mesh=mesh,
        in_specs=(
            P("xy", "zt", None, None),
            P("xy", "zt", None, None),
            P(None, "xy", "zt", None, None),
        ),
        out_specs=(P("xy", "zt", None, None), P("xy", "zt", None, None)),
        check_vma=False,
    )
```

```python
import functools

import jax
import jax.numpy as jnp
from jax import lax
from jax.experimental import pallas as pl
from jax.experimental.pallas import tpu as pltpu
from jax.sharding import PartitionSpec as P

NV = 48
RHS = 32
NT = 32
NY = 4
ROWS = 4

MESH = pl.DeviceIdType.MESH
HIGHEST = lax.Precision.HIGHEST
F32 = jnp.float32
BF16 = jnp.bfloat16

HOP_OF_SLOT = (None, 2, 3, 6, 7, 0, 1, 4, 5)
SLOTS = 9
KSLOT = 256
PITCH = 97


def dot(left, right):
    return jnp.dot(left, right, precision=HIGHEST, preferred_element_type=F32)


def lane_iota(rows):
    return lax.broadcasted_iota(jnp.int32, (rows, 128), 1)


def times_minus_i(rows):
    half = rows.shape[0] // 2
    return jnp.concatenate([rows[half:], -rows[:half]], axis=0)


def field_rows(ref, first=0):
    return ref[first : first + ROWS].reshape(ROWS * 2 * NV, 128)


def field_j(rows):
    parts = []
    for t in range(ROWS):
        base = t * 2 * NV
        parts.append(rows[base + NV : base + 2 * NV])
        parts.append(-rows[base : base + NV])
    return jnp.concatenate(parts, axis=0)


def diagonal_sum(product, tile, group):
    total = None
    for y in range(NY):
        block = product[32 * y : 32 * (y + 1), 128 * tile : 128 * (tile + 1)]
        shift = (32 * (group - y)) % 128
        if shift:
            block = pltpu.roll(block, shift, 1)
        total = block if total is None else total + block
    return total


def by_group(group, parts):
    out = parts[-1]
    for index in range(len(parts) - 2, -1, -1):
        out = jnp.where(group == index, parts[index], out)
    return out


def packed_inner(product, tiles):
    group = lane_iota(32) // 32
    return by_group(group, [diagonal_sum(product, tile, g) for g, tile in enumerate(tiles)])


def eliminate(packed):
    group = lane_iota(32) // 32
    lane = lane_iota(32)
    row32 = lax.broadcasted_iota(jnp.int32, (32, 128), 0)
    eye = jnp.where(lane == row32 + 96, 1.0, 0.0).astype(F32)
    down = pltpu.roll(packed, 96, 1)
    up = pltpu.roll(packed, 32, 1)
    top = by_group(group, [packed, -packed, packed, eye])
    bottom = by_group(group, [down, up, down, jnp.zeros_like(packed)])
    work = jnp.concatenate([top, bottom], axis=0)
    row = lax.broadcasted_iota(jnp.int32, (64, 128), 0)

    def whole(value):
        return jnp.broadcast_to(value, (8, 128))

    for k in range(0, RHS, 2):
        n = k + 1

        def at(i, j):
            return whole(work[i : i + 1, j : j + 1])

        inverse = 1.0 / at(k, k)
        first1 = whole(work[k : k + 1, :]) * inverse
        first2 = whole(work[k + 32 : k + 33, :]) * inverse
        col1, col2 = work[:, k : k + 1], work[:, k + 32 : k + 33]
        next1 = whole(work[n : n + 1, :]) - at(n, k) * first1 - at(n, k + 32) * first2
        next2 = whole(work[n + 32 : n + 33, :]) - at(n + 32, k) * first1 - at(n + 32, k + 32) * first2
        drop = at(n, k) * at(k, n) + at(n, k + 32) * at(k + 32, n)
        inverse2 = 1.0 / (at(n, n) - drop * inverse)
        second1, second2 = next1 * inverse2, next2 * inverse2
        up11, up21 = at(k, n) * inverse, at(k + 32, n) * inverse
        up12, up22 = at(k, n + 32) * inverse, at(k + 32, n + 32) * inverse
        later1 = work[:, n : n + 1] - col1 * up11[0:1] - col2 * up21[0:1]
        later2 = work[:, n + 32 : n + 33] - col1 * up12[0:1] - col2 * up22[0:1]
        updated = work - col1 * first1[0:1] - col2 * first2[0:1] - later1 * second1[0:1] - later2 * second2[0:1]
        first1, first2 = (
            first1 - up11 * second1 - up12 * second2,
            first2 - up21 * second1 - up22 * second2,
        )
        for place, value in ((k, first1), (k + 32, first2), (n, second1), (n + 32, second2)):
            updated = jnp.where(row == place, value[0:1], updated)
        work = updated
    return work


def repeated(block, group_index):
    group = lane_iota(32) // 32
    block = jnp.where(group == group_index, block, 0.0)
    block = block + pltpu.roll(block, 64, 1)
    return block + pltpu.roll(block, 32, 1)


def column_matrix(coef, group_index):
    group = lane_iota(32) // 32
    real = repeated(coef[:32], group_index)
    imag = repeated(coef[32:], group_index)
    blocks = [jnp.where(group == y, real, 0.0) for y in range(NY)]
    blocks += [jnp.where(group == y, -imag, 0.0) for y in range(NY)]
    return jnp.concatenate(blocks, axis=0)


def kernel(
    sizes,
    b_ref,
    self_ref,
    hop_ref,
    sol_ref,
    res_ref,
    raw,
    rows_scr,
    amat,
    bhi,
    blo,
    ext,
    halo,
    acc,
    second,
    pieces,
    pay,
    rs_buf,
    y_buf,
    z_buf,
    ag_buf,
    link_sem,
    b_sem,
    halo_send,
    halo_recv,
    t_send,
    t_recv,
    red_send,
    red_recv,
):
    yb, zb, xb = sizes
    zt = lax.axis_index("zt")
    xy = lax.axis_index("xy")
    my_y = lax.rem(zt, yb)
    my_z = lax.div(zt, yb)
    count = yb * zb

    def zt_at(by):
        return lax.rem(zt + (by + count), count)

    def xy_at(by):
        return lax.rem(xy + (by + xb), xb)

    def link_copies(slot):
        source = self_ref.at[0] if slot == 0 else hop_ref.at[HOP_OF_SLOT[slot], 0]
        return pltpu.make_async_copy(source, raw.at[slot], link_sem.at[slot])

    own = pltpu.make_async_copy(b_ref.at[0], ext.at[0, pl.ds(1, ROWS)], b_sem)
    own.start()
    for slot in range(SLOTS):
        link_copies(slot).start()

    partners = [(zt_at(1), xy), (zt_at(-1), xy)]
    partners += [(my_z * yb + lax.rem(my_y + o, yb), xy) for o in range(1, yb)]
    partners += [(lax.rem(my_z + o, zb) * yb + my_y, xy) for o in range(1, zb)]
    partners += [(zt, lax.rem(xy + o, xb)) for o in range(1, xb)]
    barrier = pltpu.get_barrier_semaphore()
    for partner in partners:
        pl.semaphore_signal(barrier, inc=1, device_id=partner, device_id_type=MESH)
    pl.semaphore_wait(barrier, len(partners))

    targets = ((zt, xy_at(-1)), (zt, xy_at(1)), (zt_at(-yb), xy), (zt_at(yb), xy))

    def halo_copy(which, side, t):
        return pltpu.make_async_remote_copy(
            src_ref=ext.at[which, 1 + t],
            dst_ref=halo.at[which, side, t],
            send_sem=halo_send.at[which, side, t],
            recv_sem=halo_recv.at[which, side, t],
            device_id=targets[side],
            device_id_type=MESH,
        )

    def t_copy(which, side):
        return pltpu.make_async_remote_copy(
            src_ref=ext.at[which, 1 if side == 0 else ROWS],
            dst_ref=ext.at[which, ROWS + 1 if side == 0 else 0],
            send_sem=t_send.at[which, side],
            recv_sem=t_recv.at[which, side],
            device_id=(zt_at(-1) if side == 0 else zt_at(1), xy),
            device_id_type=MESH,
        )

    own.wait()
    t_copy(0, 0).start()
    t_copy(0, 1).start()

    def start_b(t, carry):
        for side in (2, 3, 0, 1):
            halo_copy(0, side, t).start()
        return carry

    lax.fori_loop(0, ROWS, start_b, 0)

    bhi[...] = jnp.zeros_like(bhi)
    blo[...] = jnp.zeros_like(blo)
    for slot in range(SLOTS):
        link_copies(slot).wait()
    lane = lane_iota(8)
    odd = lax.rem(lax.broadcasted_iota(jnp.int32, (8, 128), 0), 2) == 1

    def relayout(step, carry):
        slot = lax.div(step, 2)
        pair = lax.rem(step, 2)
        for g in range(12):
            tiles = [
                raw[slot, pl.ds(2 * pair, 2), :, 384 * g + 128 * n : 384 * g + 128 * (n + 1)].reshape(8, 128)
                for n in range(3)
            ]
            turned = [pltpu.roll(tile, 64, 1) for tile in tiles]
            tiles = [
                jnp.where(odd, jnp.where(lane < 64, turned[n - 1], turned[n]), tiles[n]) for n in range(3)
            ]
            for r in range(8):
                n, offset = divmod(48 * r, 128)
                piece = tiles[n]
                if offset:
                    piece = jnp.where(lane < offset, tiles[(n + 1) % 3], piece)
                    piece = pltpu.roll(piece, 128 - offset, 1)
                rows_scr[pl.ds(8 * g + r, 8, stride=PITCH), :] = piece
        low = lane_iota(96) < 64
        for t in range(2):
            for h in range(2):
                base = (t * 4 + 2 * h) * PITCH
                values = jnp.where(low, rows_scr[base : base + 96, :], rows_scr[base + PITCH : base + PITCH + 96, :])
                hi = values.astype(BF16)
                lo = (values - hi.astype(F32)).astype(BF16)
                amat[2 * pair + t, slot, 0:96, 128 * h : 128 * (h + 1)] = hi
                amat[2 * pair + t, slot, 96:192, 128 * h : 128 * (h + 1)] = lo
        return carry

    lax.fori_loop(0, 2 * SLOTS, relayout, 0)

    group48 = lane_iota(48) // 32

    def put(slot, real, imag):
        for half, part in ((0, real), (1, imag)):
            hi = part.astype(BF16).astype(F32)
            lo = part - hi
            for y in range(NY):
                mask = group48 == y
                at = slice(slot * KSLOT + 64 * y, slot * KSLOT + 64 * y + 48)
                lanes = slice(128 * half, 128 * (half + 1))
                bhi[at, lanes] = jnp.where(mask, hi, 0.0).astype(BF16)
                blo[at, lanes] = jnp.where(mask, lo, 0.0).astype(BF16)

    def put_site(slot, site):
        put(slot, site[0:NV], site[NV : 2 * NV])

    def product(t, first, last):
        left = jnp.concatenate([amat[t, s] for s in range(first, last)], axis=1)
        right = slice(first * KSLOT, last * KSLOT)
        main = jnp.dot(left, bhi[right, :], preferred_element_type=F32)
        rest = jnp.dot(left[0:96], blo[right, :], preferred_element_type=F32)
        return main[0:96] + main[96:192] + rest

    def near_sites(site):
        put_site(0, -site)
        put_site(1, pltpu.roll(site, 96, 1))
        put_site(2, pltpu.roll(site, 32, 1))

    def near(which):
        def body(t, carry):
            site = ext[which, 1 + t]
            near_sites(site)
            acc[t] = product(t, 0, 3)
            return carry

        lax.fori_loop(0, ROWS, body, 0)

    def far(which, out):
        t_copy(which, 0).wait_recv()
        t_copy(which, 1).wait_recv()

        def body(t, carry):
            for side in range(4):
                halo_copy(which, side, t).wait_recv()
            put_site(3, ext[which, 2 + t])
            put_site(4, ext[which, t])
            for side in range(4):
                put_site(5 + side, halo[which, side, t])
            if which:
                total = acc[t] + product(t, 3, SLOTS)
            else:
                near_sites(ext[which, 1 + t])
                total = product(t, 0, SLOTS)
            real = total[48:96, 128:256] - total[0:48, 0:128]
            imag = -(total[48:96, 0:128] + total[0:48, 128:256])
            out(t, real, imag)
            return carry

        lax.fori_loop(0, ROWS, body, 0)

    def image_out(t, real, imag):
        ext[1, 1 + t, 0:NV, :] = real
        ext[1, 1 + t, NV : 2 * NV, :] = imag
        for side in (2, 3, 0, 1):
            halo_copy(1, side, t).start()

    far(0, image_out)
    t_copy(1, 0).start()
    t_copy(1, 1).start()

    piece = 64 // xb

    def exchange(red, phase, buffer, me, size, source, device):
        def copy(o):
            return pltpu.make_async_remote_copy(
                src_ref=source(lax.rem(me + o, size)),
                dst_ref=buffer.at[red, me],
                send_sem=red_send.at[red, phase, o],
                recv_sem=red_recv.at[red, phase, me],
                device_id=device(lax.rem(me + o, size)),
                device_id_type=MESH,
            )

        def arrival(o):
            other = lax.rem(me + o, size)
            return pltpu.make_async_remote_copy(
                src_ref=source(other),
                dst_ref=buffer.at[red, other],
                send_sem=red_send.at[red, phase, o],
                recv_sem=red_recv.at[red, phase, other],
                device_id=device(other),
                device_id_type=MESH,
            )

        def start():
            for o in range(1, size):
                copy(o).start()

        def wait():
            for o in range(1, size):
                arrival(o).wait_recv()

        def drain():
            for o in range(1, size):
                copy(o).wait_send()

        return start, wait, drain

    def y_device(other):
        return (my_z * yb + other, xy)

    def z_device(other):
        return (other * yb + my_y, xy)

    def x_device(other):
        return (zt, other)

    def reduction(red):
        scatter = exchange(red, 0, rs_buf, xy, xb, lambda other: pay.at[red, other], x_device)
        along_y = exchange(red, 1, y_buf, my_y, yb, lambda other: y_buf.at[red, my_y], y_device)
        along_z = exchange(red, 2, z_buf, my_z, zb, lambda other: z_buf.at[red, my_z], z_device)
        gather = exchange(red, 3, ag_buf, xy, xb, lambda other: ag_buf.at[red, xy], x_device)

        def summed(buffer, size):
            total = buffer[red, 0]
            for n in range(1, size):
                total = total + buffer[red, n]
            return total

        def step0(values):
            for n in range(xb):
                pay[red, n] = values[n * piece : (n + 1) * piece]
            rs_buf[red, xy] = pay[red, xy]
            scatter[0]()

        def step1():
            scatter[1]()
            y_buf[red, my_y] = summed(rs_buf, xb)
            along_y[0]()

        def step2():
            along_y[1]()
            z_buf[red, my_z] = summed(y_buf, yb)
            along_z[0]()

        def step3():
            along_z[1]()
            ag_buf[red, xy] = summed(z_buf, zb)
            gather[0]()

        def step4():
            gather[1]()
            return jnp.concatenate([ag_buf[red, n] for n in range(xb)], axis=0)

        def drain():
            for part in (scatter, along_y, along_z, gather):
                part[2]()

        return step0, step1, step2, step3, step4, drain

    red1 = reduction(0)
    red2 = reduction(1)
    group = lane_iota(32) // 32
    group64 = lane_iota(64) // 32
    zero32 = jnp.zeros((32, 128), F32)

    rhs_rows = field_rows(ext.at[0], 1)
    rhs_pair = jnp.concatenate([rhs_rows, field_j(rhs_rows)], axis=1)
    image_rows = field_rows(ext.at[1], 1)
    image_pair = jnp.concatenate([image_rows, field_j(image_rows)], axis=1)
    inner = dot(image_rows.T, jnp.concatenate([image_pair, rhs_pair], axis=1))
    packed = packed_inner(inner, (0, 1, 2, 3))
    red1[0](jnp.concatenate([packed, zero32], axis=0))

    near(1)
    red1[1]()

    def twice_out(t, real, imag):
        second[t, 0:NV, :] = real
        second[t, NV : 2 * NV, :] = imag

    far(1, twice_out)

    rhs_rows = field_rows(ext.at[0], 1)
    rhs_pair = jnp.concatenate([rhs_rows, field_j(rhs_rows)], axis=1)
    image_rows = field_rows(ext.at[1], 1)
    image_pair = jnp.concatenate([image_rows, field_j(image_rows)], axis=1)
    twice_rows = field_rows(second)
    twice_pair = jnp.concatenate([twice_rows, field_j(twice_rows)], axis=1)
    with_twice = dot(twice_rows.T, jnp.concatenate([image_pair, twice_pair, rhs_pair], axis=1))
    red2[0](
        jnp.concatenate(
            [packed_inner(with_twice, (0, 1)), packed_inner(with_twice, (2, 3, 4, 5))], axis=0
        )
    )

    def real_form(real, imag):
        top = by_group(group, [real, -pltpu.roll(imag, 32, 1), zero32, zero32])
        bottom = by_group(group, [imag, pltpu.roll(real, 32, 1), zero32, zero32])
        return jnp.concatenate([top, bottom], axis=0)

    def stacked(packed, first):
        turns = [pltpu.roll(packed, (128 - 32 * g) % 128, 1) if g else packed for g in (first, first + 1)]
        return jnp.where(group64 == 0, jnp.concatenate(turns, axis=0), 0.0)

    def form_of(column):
        return real_form(column[:32], column[32:])

    def split(values):
        hi = values.astype(BF16)
        return hi, (values - hi.astype(F32)).astype(BF16)

    def keep_pieces(index, ref, first):
        rows = field_rows(ref, first)
        hi, lo = split(jnp.concatenate([rows, field_j(rows)], axis=1))
        pieces[index, 0] = hi
        pieces[index, 1] = lo

    def combined(index, coef):
        hi, lo = split(coef)
        field_hi = pieces[index, 0]
        out = jnp.dot(field_hi, hi, preferred_element_type=F32)
        out = out + jnp.dot(pieces[index, 1], hi, preferred_element_type=F32)
        return out + jnp.dot(field_hi, lo, preferred_element_type=F32)

    red1[2]()
    red2[1]()
    keep_pieces(0, ext.at[0], 1)
    keep_pieces(1, ext.at[1], 1)
    keep_pieces(2, second, 0)
    red1[3]()
    red2[2]()
    gram = red1[4]()[0:32]
    solved = eliminate(gram)
    gram_column = stacked(gram, 0)
    gram_form = form_of(gram_column)
    target_column = stacked(gram, 2)
    coef1 = jnp.where(group64 == 0, pltpu.roll(solved, 64, 1), 0.0)
    inverse_form = form_of(pltpu.roll(solved, 32, 1))
    coef1_form = form_of(coef1)
    red2[3]()
    reduced = red2[4]()
    upper, lower = reduced[:32], reduced[32:]

    adjoint_form = form_of(stacked(upper, 0))
    cross_form = jnp.concatenate([adjoint_form, jnp.zeros_like(adjoint_form)], axis=0).T[0:64]
    image_part = gram_column - dot(cross_form[:, 0:64], coef1)
    projection = dot(inverse_form[:, 0:64], image_part)
    row64 = lax.broadcasted_iota(jnp.int32, (64, 128), 0)
    identity = jnp.where(lane_iota(64) == row64, jnp.where(group64 == 0, 1.0, 0.0), 0.0).astype(F32)
    keep = identity - projection

    grams = jnp.concatenate(
        [
            gram_form + pltpu.roll(cross_form, 64, 1),
            adjoint_form + pltpu.roll(form_of(stacked(lower, 0)), 64, 1),
        ],
        axis=0,
    )
    weights = jnp.concatenate([keep, -coef1], axis=0)
    applied = dot(grams, weights - jnp.concatenate([pltpu.roll(coef1, 64, 1), jnp.zeros_like(coef1)], axis=0))
    targets12 = jnp.concatenate([target_column, stacked(lower, 2)], axis=0)
    applied = applied + pltpu.roll(targets12, 64, 1)
    turned = jnp.concatenate([times_minus_i(applied[:64]), times_minus_i(applied[64:])], axis=0)
    applied = applied + pltpu.roll(turned, 32, 1)
    solved2 = eliminate(dot(weights.T, applied)[0:32])

    follow = dot(jnp.concatenate([form_of(keep), coef1_form], axis=0)[:, 0:64], solved2)
    step_a = column_matrix(pltpu.roll(coef1, 64, 1) + follow[:64], 2)
    step_e = column_matrix(follow[64:], 2)
    from_image = combined(1, jnp.concatenate([-step_e, -step_a], axis=1))
    sol_ref[0] = (combined(0, step_a) + from_image[:, 0:128]).reshape(ROWS, 2 * NV, 128)
    change = combined(2, step_e) + from_image[:, 128:256]
    res_ref[0] = (field_rows(ext.at[0], 1) + change).reshape(ROWS, 2 * NV, 128)

    for which in range(2):
        t_copy(which, 0).wait_send()
        t_copy(which, 1).wait_send()

    def drain(t, carry):
        for which in range(2):
            for side in range(4):
                halo_copy(which, side, t).wait_send()
        return carry

    lax.fori_loop(0, ROWS, drain, 0)
    red1[5]()
    red2[5]()


def solution(mesh):
    yb = NT // ROWS
    zb = mesh.shape["zt"] // yb
    xb = mesh.shape["xy"]
    piece = 64 // xb
    block = jax.ShapeDtypeStruct((1, ROWS, 2 * NV, 128), F32)

    def local(right_side, self_link, hop_links):
        in_hbm = pl.BlockSpec(memory_space=pltpu.HBM)
        in_vmem = pl.BlockSpec(memory_space=pltpu.VMEM)
        return pl.pallas_call(
            functools.partial(kernel, (yb, zb, xb)),
            out_shape=(block, block),
            in_specs=[in_hbm, in_hbm, in_hbm],
            out_specs=(in_vmem, in_vmem),
            scratch_shapes=[
                pltpu.VMEM((SLOTS, ROWS, NY, 2 * NV * NV), F32),
                pltpu.VMEM((8 * PITCH, 128), F32),
                pltpu.VMEM((ROWS, SLOTS, 192, KSLOT), BF16),
                pltpu.VMEM((SLOTS * KSLOT, 256), BF16),
                pltpu.VMEM((SLOTS * KSLOT, 256), BF16),
                pltpu.VMEM((2, ROWS + 2, 2 * NV, 128), F32),
                pltpu.VMEM((2, 4, ROWS, 2 * NV, 128), F32),
                pltpu.VMEM((ROWS, 96, 256), F32),
                pltpu.VMEM((ROWS, 2 * NV, 128), F32),
                pltpu.VMEM((3, 2, ROWS * 2 * NV, 256), BF16),
                pltpu.VMEM((2, xb, piece, 128), F32),
                pltpu.VMEM((2, xb, piece, 128), F32),
                pltpu.VMEM((2, yb, piece, 128), F32),
                pltpu.VMEM((2, zb, piece, 128), F32),
                pltpu.VMEM((2, xb, piece, 128), F32),
                pltpu.SemaphoreType.DMA((SLOTS,)),
                pltpu.SemaphoreType.DMA,
                pltpu.SemaphoreType.DMA((2, 4, ROWS)),
                pltpu.SemaphoreType.DMA((2, 4, ROWS)),
                pltpu.SemaphoreType.DMA((2, 2)),
                pltpu.SemaphoreType.DMA((2, 2)),
                pltpu.SemaphoreType.DMA((2, 4, 8)),
                pltpu.SemaphoreType.DMA((2, 4, 8)),
            ],
            compiler_params=pltpu.CompilerParams(
                collective_id=0, has_side_effects=True, vmem_limit_bytes=48 * 1024 * 1024
            ),
            name="two_gcr_iterations",
        )(*[pltpu.with_memory_space_constraint(x, pltpu.HBM) for x in (right_side, self_link, hop_links)])

    return jax.shard_map(
        local,
        mesh=mesh,
        in_specs=(
            P("xy", "zt", None, None),
            P("xy", "zt", None, None),
            P(None, "xy", "zt", None, None),
        ),
        out_specs=(P("xy", "zt", None, None), P("xy", "zt", None, None)),
        check_vma=False,
    )
```
